512 devices in a mesh: dp: 64 (over x, y, z_lo), node: 8 (over z_hi, core).
Axes of the slice: x: 4, y: 8, z: 8 (z_hi: 4, z_lo: 2; z = z_hi * 2 + z_lo), core: 2. Of those that a mesh axis runs over, the one named last changes fastest.
Arguments:
- hidden: bfloat16 [131072, 2048], P(('dp', 'node')), may hold values from -24 to 24
- queries: bfloat16 [131072, 1024], P(('dp', 'node')), may hold values from -64 to 64
- cotangent: bfloat16 [131072, 1024], P(('dp', 'node')), may hold values from -6 to 6
- segments: int32 [512, 256], P(('dp', 'node')), may hold values from 0 to 3, never falling along the last dimension, each value on 1 to 128 neighbouring positions
- kv_weight: bfloat16 [2048, 512], P(('dp', 'node')), may hold values from -0.125 to 0.125
Outputs:
- grad_hidden: bfloat16 [131072, 2048], P(('dp', 'node'))
- grad_weights: float32 [2048, 512], P(('dp', 'node'))
The draws below stay inside these ranges and needn't reach their ends.
Inputs may be any that keep to these rules, and one draw needn't show every extreme that they name: `segments`: within each row the segment numbers never fall.
All inputs are finite; a program needn't handle non-finite values.
Results may differ from the reference program's by a relative error of at most 0.013.
The reference program's roundings to bfloat16 on the way (of `kv`, `prob_b`, `grad_values`, `grad_scores`, `grad_keys` and `grad_kv`) count: a program that leaves them out, or rounds other values in their place, can miss the bound.
Values may be sent and summed in bfloat16 or wider, within the bound.
A program may use at most 64 MiB of HBM per device.

```python
import math
import jax
import jax.numpy as jnp
import numpy as np
from jax import lax

D = 2048
HEAD = 64
Q_HEADS = 16
KV_HEADS = 4
TOK_DEV = 256
QW = 1024
KW = 256
TOKENS = 131072
N_DP = 64
N_NODE = 8


def draw_queries(key, part):
    key = jax.random.fold_in(key, 11)
    base = jax.random.normal(key, (TOKENS, QW), jnp.float32)
    return jnp.clip(base, -64.0, 64.0).astype(jnp.bfloat16)


def with_spikes(values, rng, source, target, parts, factor):
    def block_of(dim):
        return (jnp.arange(values.shape[dim]) // (values.shape[dim] // parts)).reshape((-1,) + (1,) * (values.ndim - 1 - dim))

    one_side = jax.random.permutation(rng, parts)[block_of(target)]
    far = (block_of(target) + parts // 2) % parts
    return jnp.where((block_of(source) == one_side) | (block_of(source) == far), factor * values, values)


def steps_of(key, dims, cuts, smallest, top_value):
    gain, own = 1.0, jax.random.fold_in(key, 6)
    for dim, parts in cuts:
        draws = jnp.exp(jax.random.uniform(jax.random.fold_in(own, dim), (parts,), jnp.float32, smallest / len(cuts), top_value / len(cuts)))
        gain = gain * jnp.repeat(draws, dims[dim] // parts).reshape([-1 if axis == dim else 1 for axis in range(len(dims))])
    return gain


def length_profile(amount, total, reach, lean):
    loads = [(1 << 20) // math.isqrt(grade ** lean) + 1 for grade in range(2, amount + 1)]
    rest, given = total - reach - (amount - 1), [1] * (amount - 1)
    while rest > 0:
        movable = [i for i in range(amount - 1) if given[i] < reach]
        whole, remaining = sum([loads[i] for i in movable]), rest
        for i in movable:
            addition = min(reach - given[i], max(1, remaining * loads[i] // whole), rest)
            given[i] = given[i] + addition
            rest = rest - addition
    return np.array([reach] + given)


def uneven(key, amount, total, reach, slope):
    if amount == 2:
        one = jax.random.randint(key, (), max(1, total - reach), min(reach, total - 1) + 1)
        return jnp.stack([one, total - one])
    tallies = jnp.asarray(length_profile(amount, total, reach, slope), jnp.int32)
    couples = (amount - 1) // 2
    source_of, taker = tallies[1:1 + 2 * couples:2], tallies[2:2 + 2 * couples:2]
    slack = jnp.minimum(source_of - 1, reach - taker)
    shifted = jax.random.randint(jax.random.fold_in(key, 1), (couples,), 0, 1 << 20) % (slack + 1)
    tallies = tallies.at[1:1 + 2 * couples:2].set(source_of - shifted).at[2:2 + 2 * couples:2].set(taker + shifted)
    return tallies[jax.random.permutation(jax.random.fold_in(key, 2), amount)]


def gaussian(own_key, dims, deviation, most, split=(), kind=jnp.bfloat16):
    values = jax.random.normal(own_key, dims, jnp.float32) * deviation
    if len(split) > 0:
        values = steps_of(own_key, dims, split, -0.22, 0.18) * values
    return jnp.clip(values, min=-most, max=most).astype(kind)


def heavy_noise(own_key, shape, deviation, bound, split, heavy, held_as=jnp.bfloat16):
    array = deviation * jax.random.normal(own_key, shape, jnp.float32)
    if split:
        array = array * steps_of(own_key, shape, split, -0.22, 0.18)
    return jnp.clip(with_spikes(array, jax.random.fold_in(own_key, 3), *heavy), -bound, bound).astype(held_as)


def setup_inputs(seed: int = 0) -> dict:
    splits = jax.random.split(jax.random.key(seed), 6)
    return {
        "hidden": heavy_noise(splits[0], (TOKENS, D), 1.0, 24.0, ((0, 512),), (0, 1, 512, 6.0)),
        "queries": draw_queries(jax.random.fold_in(splits[5], 71), 0),
        "cotangent": gaussian(splits[2], (TOKENS, QW), 1.0, 6.0, ((0, 512),)),
        "segments": jax.vmap(lambda own: jnp.searchsorted(jnp.cumsum(uneven(own, 4, TOK_DEV, TOK_DEV // 2, 0)), jnp.arange(TOK_DEV), side="right"))(jax.random.split(splits[3], (N_DP * N_NODE))).reshape((N_DP * N_NODE, TOK_DEV)).astype(jnp.int32),
        "kv_weight": gaussian(splits[4], (D, 2 * KW), D ** -0.5, 0.125, ((0, 512),)),
    }


def device_block(args):
    query_rows, cot_rows, seg_row, kv_rows = args
    tok = query_rows.shape[0]
    group = Q_HEADS // KV_HEADS
    keys = kv_rows[:, :KW].reshape(tok, KV_HEADS, HEAD).astype(jnp.float32)
    values = kv_rows[:, KW:].reshape(tok, KV_HEADS, HEAD).astype(jnp.float32)
    query_f = query_rows.reshape(tok, KV_HEADS, group, HEAD).astype(jnp.float32)
    cot_f = cot_rows.reshape(tok, KV_HEADS, group, HEAD).astype(jnp.float32)
    position = jnp.arange(tok, dtype=jnp.int32)
    allowed = (seg_row[:, None] == seg_row[None, :]) & (position[:, None] >= position[None, :])
    scores = jnp.einsum('qhgd,khd->hgqk', query_f, keys) * 0.125
    scores = jnp.where(allowed, scores, -1e+30)
    top = lax.optimization_barrier(jnp.max(scores, axis=-1, keepdims=True))
    expo = jnp.exp(scores - top)
    prob = expo / lax.optimization_barrier(jnp.sum(expo, axis=-1, keepdims=True))
    prob_b = prob.astype(jnp.bfloat16).astype(jnp.float32)
    attended = jnp.einsum('hgqk,khd->qhgd', prob_b, values)
    delta = lax.optimization_barrier(jnp.sum(cot_f * attended, axis=-1))
    grad_values = jnp.einsum('hgqk,qhgd->khd', prob_b, cot_f).astype(jnp.bfloat16)
    grad_prob = jnp.einsum('qhgd,khd->hgqk', cot_f, values)
    grad_scores = (prob * (grad_prob - jnp.transpose(delta, (1, 2, 0))[..., None]) * 0.125).astype(jnp.bfloat16)
    grad_keys = jnp.einsum('hgqk,qhgd->khd', grad_scores.astype(jnp.float32), query_f).astype(jnp.bfloat16)
    return jnp.concatenate([grad_keys.reshape(tok, KW), grad_values.reshape(tok, KW)], axis=1)

def reference(hidden, queries, cotangent, segments, kv_weight):
    count = N_DP * N_NODE
    kv = jnp.dot(hidden, kv_weight, preferred_element_type=jnp.float32).astype(jnp.bfloat16)
    grad_kv = lax.map(device_block, (queries.reshape(count, TOK_DEV, QW), cotangent.reshape(count, TOK_DEV, QW), segments, kv.reshape(count, TOK_DEV, 2 * KW)))
    grad_kv = grad_kv.reshape(count * TOK_DEV, 2 * KW)
    grad_hidden = lax.dot_general(grad_kv, kv_weight, (((1,), (1,)), ((), ())), preferred_element_type=jnp.float32).astype(jnp.bfloat16)
    summed = lax.dot_general(hidden, grad_kv, (((0,), (0,)), ((), ())), preferred_element_type=jnp.float32)
    grad_weights = summed * (1.0 / math.sqrt(count * TOK_DEV))
    return (grad_hidden, grad_weights)
```

```python
import functools
import math

import jax
import jax.numpy as jnp
from jax import lax
from jax.experimental import pallas as pl
from jax.experimental.pallas import tpu as pltpu
from jax.sharding import PartitionSpec as P

HEAD = 64
KV_HEADS = 4
GROUP = 4
TOK = 256
HALF = 128
NX, NY, NZL, NZH, NC = 4, 8, 2, 4, 2
NZC = 16
CH = KV_HEADS
MESH = pl.DeviceIdType.MESH
F32, BF16 = jnp.float32, jnp.bfloat16
NT = (((1,), (1,)), ((), ()))
NEAR = (1, 7, 2, 6, 3, 5, 4)


def dot(a, b):
    return jnp.dot(a, b, preferred_element_type=F32)


def natural(w_ref, j, x):
    both = jnp.stack([w_ref[j, 0, x], w_ref[j, 1, x]], axis=1)
    return both.reshape(512, 128)


def kernel(
    scale,
    hid_hbm, que_hbm, cot_hbm, seg_hbm, kvw_hbm,
    gh_hbm, gw_ref,
    hid, que, cot, seg, kvw,
    blk, zrecv, w, h_t, q_t, c_t, q_n, c_n, bias_a, bias_b,
    s_a, s_b, d_a, d_b, p_a, p_b, ds_a, ds_b, gkv,
    g_send, c_recv, x_send, x_recv, y_send, y_recv, z_sum, z_send, f_recv, gh,
    in_sem, out_sem,
    az_s, az_r, ay_s, ay_r, ax_s, ax_r, ac_s, ac_r,
    rc_s, rc_r, rx_s, rx_r, ry_s, ry_r, rz_s, rz_r,
):
    dp, node = lax.axis_index("dp"), lax.axis_index("node")
    x = dp // (NY * NZL)
    y = (dp // NZL) % NY
    zl = dp % NZL
    zh = node // NC
    core = node % NC
    z = zh * NZL + zl

    def at(x_, y_, z_, c_):
        return ((x_ * NY + y_) * NZL + z_ % NZL, (z_ // NZL) * NC + c_)

    ins = [
        pltpu.make_async_copy(kvw_hbm, kvw, in_sem.at[0]),
        pltpu.make_async_copy(hid_hbm, hid, in_sem.at[1]),
        pltpu.make_async_copy(que_hbm, que, in_sem.at[2]),
        pltpu.make_async_copy(cot_hbm, cot, in_sem.at[3]),
        pltpu.make_async_copy(seg_hbm, seg, in_sem.at[4]),
    ]
    for cp in ins:
        cp.start()

    barrier = pltpu.get_barrier_semaphore()

    def greet_z(k, carry):
        other = (z * NC + core + k) % NZC
        pl.semaphore_signal(
            barrier, inc=1, device_id=at(x, y, other // NC, other % NC), device_id_type=MESH
        )
        return carry

    def greet_y(k, carry):
        pl.semaphore_signal(
            barrier, inc=1, device_id=at(x, (y + k) % NY, z, core), device_id_type=MESH
        )
        return carry

    def greet_x(k, carry):
        pl.semaphore_signal(
            barrier, inc=1, device_id=at((x + k) % NX, y, z, core), device_id_type=MESH
        )
        return carry

    lax.fori_loop(1, NZC, greet_z, 0)
    lax.fori_loop(1, NY, greet_y, 0)
    lax.fori_loop(1, NX, greet_x, 0)

    ins[0].wait()
    own = kvw[...].astype(F32)
    blk[...] = jnp.concatenate(
        [
            jnp.concatenate([own[:, j * 64 : j * 64 + 64], own[:, 256 + j * 64 : 320 + j * 64]], axis=1)
            for j in range(CH)
        ],
        axis=0,
    ).astype(BF16)
    pl.semaphore_wait(barrier, (NZC - 1) + (NY - 1) + (NX - 1))

    slot = zh * NC + core

    def gather_z(a, b, remote):
        if not remote:
            return pltpu.make_async_copy(blk, zrecv.at[slot], az_r)
        return pltpu.make_async_remote_copy(
            blk, zrecv.at[slot], az_s, az_r,
            device_id=at(x, y, ((zh + a) % NZH) * NZL + (zl + b) % NZL, zl), device_id_type=MESH,
        )

    for a in range(NZH):
        for b in range(NZL):
            if a or b:
                gather_z(a, b, True).start()
    home = core == zl

    @pl.when(home)
    def _():
        gather_z(0, 0, False).start()

    @pl.when(jnp.logical_not(home))
    def _():
        gather_z(0, 0, True).start()

    ins[1].wait()
    for t in range(16):
        cols = hid[:, t * 128 : (t + 1) * 128].astype(F32)
        turned = jnp.transpose(cols).astype(BF16)
        for half in range(4):
            row = t * 2 + half // 2
            h_t[half % 2, row * 32 : row * 32 + 32, :] = turned[half * 32 : half * 32 + 32, :]

    pltpu.make_async_copy(zrecv, zrecv, az_r).wait()
    r_out = lax.broadcasted_iota(jnp.int32, (128, 128), 0)
    r_in = lax.broadcasted_iota(jnp.int32, (128, 128), 1)
    wanted = ((r_out // 4) % 8) * 16 + (r_out // 32) * 4 + r_out % 4
    mine = dot((r_in == wanted).astype(BF16), zrecv[...].reshape(128, 128)).astype(BF16)
    w[:, core, x, y] = mine.reshape(CH, 32, 128)

    def copy_y(j, k):
        return pltpu.make_async_remote_copy(
            w.at[j, core, x, y], w.at[j, core, x, y], ay_s, ay_r.at[j, k - 1],
            device_id=at(x, (y + k) % NY, z, core), device_id_type=MESH,
        )

    def wait_y(j, k):
        src = (y + NY - k) % NY
        pltpu.make_async_copy(
            w.at[j, core, x, src], w.at[j, core, x, src], ay_r.at[j, k - 1]
        ).wait()

    def copy_x(j, yb, a):
        return pltpu.make_async_remote_copy(
            w.at[j, core, x, yb], w.at[j, core, x, yb], ax_s, ax_r.at[j],
            device_id=at((x + a) % NX, y, z, core), device_id_type=MESH,
        )

    def send_y(j, carry):
        for k in NEAR:
            copy_y(j, k).start()
        for a in (2, 1, 3):
            copy_x(j, y, a).start()
        return carry

    lax.fori_loop(0, CH, send_y, 0)

    ins[2].wait()
    ins[3].wait()
    lane = lax.broadcasted_iota(jnp.int32, (TOK, 128), 1)
    low = lane < 64
    zeros = jnp.zeros((64, 512), BF16)
    for j in range(CH):
        for part in range(2):
            q_t[j, part, 64:128, :] = zeros
            c_t[j, part, 0:64, :] = zeros
        for pair in range(2):
            tile = j * 2 + pair
            q = que[:, tile * 128 : (tile + 1) * 128].astype(F32) * 0.125
            c = cot[:, tile * 128 : (tile + 1) * 128].astype(F32)
            q_turn, c_turn = jnp.transpose(q).astype(BF16), jnp.transpose(c).astype(BF16)
            q_swap, c_swap = pltpu.roll(q, 64, 1), pltpu.roll(c, 64, 1)
            q_rows = (jnp.where(low, q, 0.0).astype(BF16), jnp.where(low, q_swap, 0.0).astype(BF16))
            c_rows = (jnp.where(low, 0.0, c_swap).astype(BF16), jnp.where(low, 0.0, c).astype(BF16))
            for side in range(2):
                g = pair * 2 + side
                for part in range(2):
                    toks = slice(part * 128, part * 128 + 128)
                    lanes = slice(g * 128, g * 128 + 128)
                    q_t[j, part, 0:64, lanes] = q_turn[side * 64 : side * 64 + 64, toks]
                    c_t[j, part, 64:128, lanes] = c_turn[side * 64 : side * 64 + 64, toks]
                    q_n[j, part, lanes, :] = q_rows[side][toks, :]
                    c_n[j, part, lanes, :] = c_rows[side][toks, :]

    def forward(j, carry):
        for k in NEAR:
            wait_y(j, k)
            for a in (2, 1, 3):
                copy_x(j, (y + NY - k) % NY, a).start()
        return carry

    lax.fori_loop(0, CH, forward, 0)

    ins[4].wait()
    seg_i = jnp.broadcast_to(seg[...].astype(F32), (TOK, TOK))
    seg_j = jnp.transpose(seg_i)
    pos_j = lax.broadcasted_iota(jnp.int32, (TOK, TOK), 0)
    pos_i = lax.broadcasted_iota(jnp.int32, (TOK, TOK), 1)
    bias = jnp.where((seg_i == seg_j) & (pos_i >= pos_j), 0.0, -1e30)
    bias_a[...] = bias[0:128, 0:128]
    bias_b[...] = bias[:, 128:256]

    def wait_x(j):
        pltpu.make_async_copy(w.at[j, core, 0:3], w.at[j, core, 0:3], ax_r.at[j]).wait()

    def other_core():
        return at(x, y, z, 1 - core)

    def copy_core(j):
        return pltpu.make_async_remote_copy(
            w.at[j, core], w.at[j, core], ac_s, ac_r.at[j],
            device_id=other_core(), device_id_type=MESH,
        )

    def wait_core(j):
        pltpu.make_async_copy(w.at[j, 1 - core], w.at[j, 1 - core], ac_r.at[j]).wait()

    wait_x(0)
    copy_core(0).start()

    def heads(s_ref, d_ref, b_ref, p_ref, o_ref):
        def one(g, carry):
            lanes = pl.ds(pl.multiple_of(g * 128, 128), 128)
            s = s_ref[:, lanes] + b_ref[...]
            e = jnp.exp(s - jnp.max(s, axis=0, keepdims=True))
            p = e * (1.0 / jnp.sum(e, axis=0, keepdims=True))
            pb = p.astype(BF16)
            d = d_ref[:, lanes]
            delta = jnp.sum(pb.astype(F32) * d, axis=0, keepdims=True)
            p_ref[:, lanes] = pb
            o_ref[:, lanes] = (p * (d - delta)).astype(BF16)
            return carry

        lax.fori_loop(0, GROUP, one, 0)

    def copy_rc(j):
        return pltpu.make_async_remote_copy(
            g_send.at[j], c_recv.at[j], rc_s, rc_r.at[j],
            device_id=other_core(), device_id_type=MESH,
        )

    def copy_rx(j, a):
        to = (x + a) % NX
        return pltpu.make_async_remote_copy(
            x_send.at[j, to], x_recv.at[j, a - 1], rx_s, rx_r.at[j],
            device_id=at(to, y, z, core), device_id_type=MESH,
        )

    def copy_ry(j, k):
        to = (y + k) % NY
        return pltpu.make_async_remote_copy(
            y_send.at[j, to], y_recv.at[j, k - 1], ry_s, ry_r.at[j],
            device_id=at(x, to, z, core), device_id_type=MESH,
        )

    def take_x(j):
        pltpu.make_async_copy(x_recv.at[j], x_recv.at[j], rx_r.at[j]).wait()
        total = x_send[j, x].astype(F32)
        for a in range(NX - 1):
            total += x_recv[j, a].astype(F32)
        y_send[j] = total.astype(BF16)
        for k in (4, 3, 5, 2, 6, 1, 7):
            copy_ry(j, k).start()

    def take_y(j):
        pltpu.make_async_copy(y_recv.at[j], y_recv.at[j], ry_r.at[j]).wait()
        total = y_send[j, y].astype(F32)
        for k in range(NY - 1):
            total += y_recv[j, k].astype(F32)
        z_sum[j] = total.astype(BF16)

    def chunk(j, carry):
        wait_core(j)
        kv = jnp.zeros((TOK, 128), F32)
        for xx in range(NX):
            kv += dot(hid[:, xx * 512 : (xx + 1) * 512], natural(w, j, xx))
        kv = kv.astype(BF16)
        s_a[...] = dot(kv[0:128], q_t[j, 0])
        d_a[...] = dot(kv[0:128], c_t[j, 0])
        s_b[...] = dot(kv, q_t[j, 1])
        d_b[...] = dot(kv, c_t[j, 1])
        heads(s_a, d_a, bias_a, p_a, ds_a)
        heads(s_b, d_b, bias_b, p_b, ds_b)
        late = dot(ds_b[...], q_n[j, 1]) + dot(p_b[...], c_n[j, 1])
        early = dot(ds_a[...], q_n[j, 0]) + dot(p_a[...], c_n[j, 0])
        grad = jnp.concatenate([late[0:128] + early, late[128:256]], axis=0).astype(BF16)
        gkv[j] = grad
        g_send[j] = dot(h_t[1 - core], grad).astype(BF16).reshape(NX, NY, 32, 128)
        copy_rc(j).start()

        @pl.when(j < CH - 1)
        def _():
            wait_x(j + 1)
            copy_core(j + 1).start()

        @pl.when(j >= 2)
        def _():
            take_x(j - 2)

        pltpu.make_async_copy(c_recv.at[j], c_recv.at[j], rc_r.at[j]).wait()
        part = dot(h_t[core], gkv[j]).reshape(NX, NY, 32, 128) + c_recv[j].astype(F32)
        x_send[j] = part.astype(BF16)
        for a in (2, 1, 3):
            copy_rx(j, a).start()
        return carry

    lax.fori_loop(0, CH, chunk, 0)

    take_x(CH - 2)
    grads = jnp.concatenate([gkv[j] for j in range(CH)], axis=1)

    def hidden_part(xx, carry):
        rows = jnp.concatenate([natural(w, j, xx) for j in range(CH)], axis=1)
        cols = pl.ds(pl.multiple_of(xx * 512, 512), 512)
        gh[:, cols] = lax.dot_general(grads, rows, NT, preferred_element_type=F32).astype(BF16)
        return carry

    lax.fori_loop(0, NX, hidden_part, 0)
    out = pltpu.make_async_copy(gh, gh_hbm, out_sem)
    out.start()

    take_x(CH - 1)
    lax.fori_loop(0, CH, lambda j, carry: (take_y(j), carry)[1], 0)

    back = ((r_out % 16) // 4) * 32 + (r_out // 16) * 4 + r_out % 4
    z_send[...] = (
        dot((r_in == back).astype(BF16), z_sum[...].reshape(128, 128)).astype(BF16).reshape(8, 16, 128)
    )

    def scatter_z(a, b, remote):
        to_h, to_c = (zh + a) % NZH, (core + b) % NC
        piece = z_send.at[to_h * NC + to_c]
        if not remote:
            return pltpu.make_async_copy(piece, f_recv.at[z], rz_r)
        return pltpu.make_async_remote_copy(
            piece, f_recv.at[z], rz_s, rz_r,
            device_id=at(x, y, to_h * NZL + core, to_c), device_id_type=MESH,
        )

    for a in (2, 1, 3, 0):
        for b in range(NC):
            if a or b:
                scatter_z(a, b, True).start()

    @pl.when(home)
    def _():
        scatter_z(0, 0, False).start()

    @pl.when(jnp.logical_not(home))
    def _():
        scatter_z(0, 0, True).start()

    pltpu.make_async_copy(zrecv.at[0:7], zrecv.at[0:7], az_s).wait()

    @pl.when(jnp.logical_not(home))
    def _():
        pltpu.make_async_copy(zrecv.at[0], zrecv.at[0], az_s).wait()

    pltpu.make_async_copy(y_recv, y_recv, ay_s).wait()
    pltpu.make_async_copy(x_recv, x_recv, ax_s).wait()
    pltpu.make_async_copy(c_recv, c_recv, ac_s).wait()
    pltpu.make_async_copy(c_recv, c_recv, rc_s).wait()
    pltpu.make_async_copy(x_recv, x_recv, rx_s).wait()
    pltpu.make_async_copy(y_recv, y_recv, ry_s).wait()
    out.wait()

    pltpu.make_async_copy(f_recv, f_recv, rz_r).wait()
    total = f_recv[0].astype(F32)
    for k in range(1, 8):
        total += f_recv[k].astype(F32)
    gw_ref[...] = total * scale

    pltpu.make_async_copy(f_recv.at[0:7], f_recv.at[0:7], rz_s).wait()

    @pl.when(jnp.logical_not(home))
    def _():
        pltpu.make_async_copy(f_recv.at[0], f_recv.at[0], rz_s).wait()


def on_device(hidden, queries, cotangent, segments, kv_weight):
    any_space = pl.BlockSpec(memory_space=pl.ANY)
    vmem = pl.BlockSpec(memory_space=pltpu.VMEM)
    scale = 1.0 / math.sqrt(lax.axis_size(("dp", "node")) * TOK)
    dma = pltpu.SemaphoreType.DMA
    scratch = [
        ((TOK, 2048), BF16), ((TOK, 1024), BF16), ((TOK, 1024), BF16), ((1, TOK), jnp.int32), ((4, 512), BF16),
        ((16, 128), BF16), ((8, 16, 128), BF16), ((CH, 2, NX, NY, 32, 128), BF16), ((2, 1024, TOK), BF16),
        ((CH, 2, 128, 512), BF16), ((CH, 2, 128, 512), BF16), ((CH, 2, 512, 128), BF16), ((CH, 2, 512, 128), BF16),
        ((128, 128), F32), ((256, 128), F32),
        ((128, 512), F32), ((256, 512), F32), ((128, 512), F32), ((256, 512), F32),
        ((128, 512), BF16), ((256, 512), BF16), ((128, 512), BF16), ((256, 512), BF16), ((CH, TOK, 128), BF16),
        ((CH, NX, NY, 32, 128), BF16), ((CH, NX, NY, 32, 128), BF16),
        ((CH, NX, NY, 32, 128), BF16), ((CH, NX - 1, NY, 32, 128), BF16),
        ((CH, NY, 32, 128), BF16), ((CH, NY - 1, 32, 128), BF16),
        ((CH, 32, 128), BF16), ((8, 16, 128), BF16), ((8, 16, 128), BF16), ((TOK, 2048), BF16),
    ]
    grad_hidden, packed = pl.pallas_call(
        functools.partial(kernel, scale),
        out_shape=(
            jax.ShapeDtypeStruct((TOK, 2048), BF16),
            jax.ShapeDtypeStruct((16, 128), F32),
        ),
        in_specs=[any_space] * 5,
        out_specs=(any_space, vmem),
        scratch_shapes=[pltpu.VMEM(shape, kind) for shape, kind in scratch]
        + [
            dma((5,)), dma,
            dma, dma, dma, dma((CH, NY - 1)), dma, dma((CH,)), dma, dma((CH,)),
            dma, dma((CH,)), dma, dma((CH,)), dma, dma((CH,)), dma, dma,
        ],
        compiler_params=pltpu.CompilerParams(
            collective_id=0, has_side_effects=True, vmem_limit_bytes=48 << 20
        ),
    )(hidden, queries, cotangent, segments, kv_weight)
    grad_weights = packed.reshape(CH, 4, 2, 64).transpose(1, 2, 0, 3).reshape(4, 512)
    return grad_hidden, grad_weights


def solution(mesh):
    placed = P(("dp", "node"), None)
    return jax.shard_map(
        on_device,
        mesh=mesh,
        in_specs=(placed,) * 5,
        out_specs=(placed, placed),
        check_vma=False,
    )
```

```python
import functools
import math

import jax
import jax.numpy as jnp
from jax import lax
from jax.experimental import pallas as pl
from jax.experimental.pallas import tpu as pltpu
from jax.sharding import PartitionSpec as P

HEAD = 64
KV_HEADS = 4
GROUP = 4
TOK = 256
HALF = 128
NX, NY, NZL, NZH, NC = 4, 8, 2, 4, 2
NZC = 16
CH = KV_HEADS
MESH = pl.DeviceIdType.MESH
F32, BF16 = jnp.float32, jnp.bfloat16
NT = (((1,), (1,)), ((), ()))
NEAR = (1, 7, 2, 6, 3, 5, 4)
FAR = (4, 3, 5, 2, 6, 1, 7, 0)
LAST = CH - 1


def dot(a, b):
    return jnp.dot(a, b, preferred_element_type=F32)


def natural(w_ref, j, x):
    both = jnp.stack([w_ref[j, 0, x], w_ref[j, 1, x]], axis=1)
    return both.reshape(512, 128)


def kernel(
    scale,
    hid_hbm, que_hbm, cot_hbm, seg_hbm, kvw_hbm,
    gh_hbm, gw_ref,
    hid, que, cot, seg, kvw,
    blk, zrecv, w, h_t, q_t, c_t, q_n, c_n, bias_a, bias_b,
    s_a, s_b, d_a, d_b, p_a, p_b, ds_a, ds_b, gkv,
    g_send, c_recv, x_send, x_recv, y_send, y_recv, z_sum, z_send, f_recv, gh,
    in_sem, out_sem,
    az_s, az_r, ay_s, ay_r, ax_s, ax_r, bx_s, bx_r, by_s, by_r, ac_s, ac_r,
    rc_s, rc_r, rx_s, rx_r, ry_s, ry_r, rz_s, rz_r,
):
    dp, node = lax.axis_index("dp"), lax.axis_index("node")
    x = dp // (NY * NZL)
    y = (dp // NZL) % NY
    zl = dp % NZL
    zh = node // NC
    core = node % NC
    z = zh * NZL + zl

    def at(x_, y_, z_, c_):
        return ((x_ * NY + y_) * NZL + z_ % NZL, (z_ // NZL) * NC + c_)

    ins = [
        pltpu.make_async_copy(kvw_hbm, kvw, in_sem.at[0]),
        pltpu.make_async_copy(hid_hbm, hid, in_sem.at[1]),
        pltpu.make_async_copy(que_hbm, que, in_sem.at[2]),
        pltpu.make_async_copy(cot_hbm, cot, in_sem.at[3]),
        pltpu.make_async_copy(seg_hbm, seg, in_sem.at[4]),
    ]
    for cp in ins:
        cp.start()

    barrier = pltpu.get_barrier_semaphore()

    def greet_z(k, carry):
        other = (z * NC + core + k) % NZC
        pl.semaphore_signal(
            barrier, inc=1, device_id=at(x, y, other // NC, other % NC), device_id_type=MESH
        )
        return carry

    def greet_y(k, carry):
        pl.semaphore_signal(
            barrier, inc=1, device_id=at(x, (y + k) % NY, z, core), device_id_type=MESH
        )
        return carry

    def greet_x(k, carry):
        pl.semaphore_signal(
            barrier, inc=1, device_id=at((x + k) % NX, y, z, core), device_id_type=MESH
        )
        return carry

    lax.fori_loop(1, NZC, greet_z, 0)
    lax.fori_loop(1, NY, greet_y, 0)
    lax.fori_loop(1, NX, greet_x, 0)

    ins[0].wait()
    own = kvw[...].astype(F32)
    blk[...] = jnp.concatenate(
        [
            jnp.concatenate([own[:, j * 64 : j * 64 + 64], own[:, 256 + j * 64 : 320 + j * 64]], axis=1)
            for j in range(CH)
        ],
        axis=0,
    ).astype(BF16)
    pl.semaphore_wait(barrier, (NZC - 1) + (NY - 1) + (NX - 1))

    slot = zh * NC + core

    def gather_z(a, b, remote):
        if not remote:
            return pltpu.make_async_copy(blk, zrecv.at[slot], az_r)
        return pltpu.make_async_remote_copy(
            blk, zrecv.at[slot], az_s, az_r,
            device_id=at(x, y, ((zh + a) % NZH) * NZL + (zl + b) % NZL, zl), device_id_type=MESH,
        )

    for a in range(NZH):
        for b in range(NZL):
            if a or b:
                gather_z(a, b, True).start()
    home = core == zl

    @pl.when(home)
    def _():
        gather_z(0, 0, False).start()

    @pl.when(jnp.logical_not(home))
    def _():
        gather_z(0, 0, True).start()

    ins[1].wait()
    for t in range(16):
        cols = hid[:, t * 128 : (t + 1) * 128].astype(F32)
        turned = jnp.transpose(cols).astype(BF16)
        for half in range(4):
            row = t * 2 + half // 2
            h_t[half % 2, row * 32 : row * 32 + 32, :] = turned[half * 32 : half * 32 + 32, :]

    pltpu.make_async_copy(zrecv, zrecv, az_r).wait()
    r_out = lax.broadcasted_iota(jnp.int32, (128, 128), 0)
    r_in = lax.broadcasted_iota(jnp.int32, (128, 128), 1)
    wanted = ((r_out // 4) % 8) * 16 + (r_out // 32) * 4 + r_out % 4
    mine = dot((r_in == wanted).astype(BF16), zrecv[...].reshape(128, 128)).astype(BF16)
    w[:, core, x, y] = mine.reshape(CH, 32, 128)

    def copy_y(j, k):
        return pltpu.make_async_remote_copy(
            w.at[j, core, x, y], w.at[j, core, x, y], ay_s, ay_r.at[j, k - 1],
            device_id=at(x, (y + k) % NY, z, core), device_id_type=MESH,
        )

    def first_x(a):
        return pltpu.make_async_remote_copy(
            w.at[LAST, core, x, y], w.at[LAST, core, x, y], bx_s, bx_r.at[a - 1],
            device_id=at((x + a) % NX, y, z, core), device_id_type=MESH,
        )

    def wait_first_x(a):
        src = (x + NX - a) % NX
        pltpu.make_async_copy(
            w.at[LAST, core, src, y], w.at[LAST, core, src, y], bx_r.at[a - 1]
        ).wait()

    def then_y(xb, k):
        return pltpu.make_async_remote_copy(
            w.at[LAST, core, xb, y], w.at[LAST, core, xb, y], by_s, by_r,
            device_id=at(x, (y + k) % NY, z, core), device_id_type=MESH,
        )

    def wait_y(j, k):
        src = (y + NY - k) % NY
        pltpu.make_async_copy(
            w.at[j, core, x, src], w.at[j, core, x, src], ay_r.at[j, k - 1]
        ).wait()

    def copy_x(j, yb, a):
        return pltpu.make_async_remote_copy(
            w.at[j, core, x, yb], w.at[j, core, x, yb], ax_s, ax_r.at[j],
            device_id=at((x + a) % NX, y, z, core), device_id_type=MESH,
        )

    def send_y(j, carry):
        for k in NEAR:
            copy_y(j, k).start()
        for a in (2, 1, 3):
            copy_x(j, y, a).start()
        return carry

    lax.fori_loop(0, 1, send_y, 0)
    for a in (2, 1, 3):
        first_x(a).start()
    lax.fori_loop(1, LAST, send_y, 0)
    for k in NEAR:
        then_y(x, k).start()

    ins[2].wait()
    ins[3].wait()
    lane = lax.broadcasted_iota(jnp.int32, (TOK, 128), 1)
    low = lane < 64
    zeros = jnp.zeros((64, 512), BF16)
    for j in range(CH):
        for part in range(2):
            q_t[j, part, 64:128, :] = zeros
            c_t[j, part, 0:64, :] = zeros
        for pair in range(2):
            tile = j * 2 + pair
            q = que[:, tile * 128 : (tile + 1) * 128].astype(F32) * 0.125
            c = cot[:, tile * 128 : (tile + 1) * 128].astype(F32)
            q_turn, c_turn = jnp.transpose(q).astype(BF16), jnp.transpose(c).astype(BF16)
            q_swap, c_swap = pltpu.roll(q, 64, 1), pltpu.roll(c, 64, 1)
            q_rows = (jnp.where(low, q, 0.0).astype(BF16), jnp.where(low, q_swap, 0.0).astype(BF16))
            c_rows = (jnp.where(low, 0.0, c_swap).astype(BF16), jnp.where(low, 0.0, c).astype(BF16))
            for side in range(2):
                g = pair * 2 + side
                for part in range(2):
                    toks = slice(part * 128, part * 128 + 128)
                    lanes = slice(g * 128, g * 128 + 128)
                    q_t[j, part, 0:64, lanes] = q_turn[side * 64 : side * 64 + 64, toks]
                    c_t[j, part, 64:128, lanes] = c_turn[side * 64 : side * 64 + 64, toks]
                    q_n[j, part, lanes, :] = q_rows[side][toks, :]
                    c_n[j, part, lanes, :] = c_rows[side][toks, :]

    def forward(j, carry):
        for k in NEAR:
            wait_y(j, k)
            for a in (2, 1, 3):
                copy_x(j, (y + NY - k) % NY, a).start()
        return carry

    lax.fori_loop(0, 1, forward, 0)
    for a in (1, 3, 2):
        wait_first_x(a)
        for k in NEAR:
            then_y((x + NX - a) % NX, k).start()
    lax.fori_loop(1, LAST, forward, 0)

    ins[4].wait()
    seg_i = jnp.broadcast_to(seg[...].astype(F32), (TOK, TOK))
    seg_j = jnp.transpose(seg_i)
    pos_j = lax.broadcasted_iota(jnp.int32, (TOK, TOK), 0)
    pos_i = lax.broadcasted_iota(jnp.int32, (TOK, TOK), 1)
    bias = jnp.where((seg_i == seg_j) & (pos_i >= pos_j), 0.0, -1e30)
    bias_a[...] = bias[0:128, 0:128]
    bias_b[...] = bias[:, 128:256]

    def wait_x(j):
        pltpu.make_async_copy(w.at[j, core, 0:3], w.at[j, core, 0:3], ax_r.at[j]).wait()

    def wait_then_y():
        blocks = w.at[LAST, core, :, 0 : NY - 1]
        pltpu.make_async_copy(blocks, blocks, by_r).wait()

    def other_core():
        return at(x, y, z, 1 - core)

    def copy_core(j):
        return pltpu.make_async_remote_copy(
            w.at[j, core], w.at[j, core], ac_s, ac_r.at[j],
            device_id=other_core(), device_id_type=MESH,
        )

    def wait_core(j):
        pltpu.make_async_copy(w.at[j, 1 - core], w.at[j, 1 - core], ac_r.at[j]).wait()

    wait_x(0)
    copy_core(0).start()

    def heads(s_ref, d_ref, b_ref, p_ref, o_ref):
        for g in range(GROUP):
            lanes = slice(g * 128, g * 128 + 128)
            s = s_ref[:, lanes] + b_ref[...]
            e = jnp.exp(s - jnp.max(s, axis=0, keepdims=True))
            p = e * (1.0 / jnp.sum(e, axis=0, keepdims=True))
            pb = p.astype(BF16)
            d = d_ref[:, lanes]
            delta = jnp.sum(pb.astype(F32) * d, axis=0, keepdims=True)
            p_ref[:, lanes] = pb
            o_ref[:, lanes] = (p * (d - delta)).astype(BF16)

    def copy_rc(j):
        return pltpu.make_async_remote_copy(
            g_send.at[j], c_recv.at[j], rc_s, rc_r.at[j],
            device_id=other_core(), device_id_type=MESH,
        )

    def copy_rx(j, k, a):
        to, yb = (x + a) % NX, (y + k) % NY
        return pltpu.make_async_remote_copy(
            x_send.at[j, to, yb], x_recv.at[j, a - 1, yb], rx_s, rx_r.at[j, k],
            device_id=at(to, y, z, core), device_id_type=MESH,
        )

    def copy_ry(j, k):
        to = (y + k) % NY
        return pltpu.make_async_remote_copy(
            y_send.at[j, to], y_recv.at[j, k - 1], ry_s, ry_r.at[j],
            device_id=at(x, to, z, core), device_id_type=MESH,
        )

    def take_x(j):
        for k in FAR:
            yb = (y + k) % NY
            blocks = x_recv.at[j, :, yb]
            pltpu.make_async_copy(blocks, blocks, rx_r.at[j, k]).wait()
            total = x_send[j, x, yb].astype(F32)
            for a in range(NX - 1):
                total += x_recv[j, a, yb].astype(F32)
            y_send[j, yb] = total.astype(BF16)
            if k:
                copy_ry(j, k).start()

    def take_y(j):
        pltpu.make_async_copy(y_recv.at[j], y_recv.at[j], ry_r.at[j]).wait()
        total = y_send[j, y].astype(F32)
        for k in range(NY - 1):
            total += y_recv[j, k].astype(F32)
        z_sum[j] = total.astype(BF16)

    def chunk(j, carry):
        wait_core(j)
        kv = jnp.zeros((TOK, 128), F32)
        for xx in range(NX):
            kv += dot(hid[:, xx * 512 : (xx + 1) * 512], natural(w, j, xx))
        kv = kv.astype(BF16)
        s_a[...] = dot(kv[0:128], q_t[j, 0])
        d_a[...] = dot(kv[0:128], c_t[j, 0])
        s_b[...] = dot(kv, q_t[j, 1])
        d_b[...] = dot(kv, c_t[j, 1])
        heads(s_a, d_a, bias_a, p_a, ds_a)
        heads(s_b, d_b, bias_b, p_b, ds_b)

        @pl.when(j < LAST - 1)
        def _():
            wait_x(j + 1)
            copy_core(j + 1).start()

        @pl.when(j == LAST - 1)
        def _():
            wait_then_y()
            copy_core(LAST).start()

        late = dot(ds_b[...], q_n[j, 1]) + dot(p_b[...], c_n[j, 1])
        early = dot(ds_a[...], q_n[j, 0]) + dot(p_a[...], c_n[j, 0])
        grad = jnp.concatenate([late[0:128] + early, late[128:256]], axis=0).astype(BF16)
        gkv[j] = grad
        g_send[j] = dot(h_t[1 - core], grad).astype(BF16).reshape(NX, NY, 32, 128)
        copy_rc(j).start()

        @pl.when(j >= 2)
        def _():
            take_x(j - 2)

        pltpu.make_async_copy(c_recv.at[j], c_recv.at[j], rc_r.at[j]).wait()
        part = dot(h_t[core], gkv[j]).reshape(NX, NY, 32, 128) + c_recv[j].astype(F32)
        x_send[j] = part.astype(BF16)
        for k in FAR:
            for a in (2, 1, 3):
                copy_rx(j, k, a).start()
        return carry

    lax.fori_loop(0, CH, chunk, 0)

    take_x(CH - 2)
    grads = jnp.concatenate([gkv[j] for j in range(CH)], axis=1)

    def hidden_part(xx, carry):
        rows = jnp.concatenate([natural(w, j, xx) for j in range(CH)], axis=1)
        cols = pl.ds(pl.multiple_of(xx * 512, 512), 512)
        gh[:, cols] = lax.dot_general(grads, rows, NT, preferred_element_type=F32).astype(BF16)
        return carry

    lax.fori_loop(0, NX, hidden_part, 0)
    out = pltpu.make_async_copy(gh, gh_hbm, out_sem)
    out.start()

    take_x(CH - 1)
    lax.fori_loop(0, CH, lambda j, carry: (take_y(j), carry)[1], 0)

    back = ((r_out % 16) // 4) * 32 + (r_out // 16) * 4 + r_out % 4
    z_send[...] = (
        dot((r_in == back).astype(BF16), z_sum[...].reshape(128, 128)).astype(BF16).reshape(8, 16, 128)
    )

    def scatter_z(a, b, remote):
        to_h, to_c = (zh + a) % NZH, (core + b) % NC
        piece = z_send.at[to_h * NC + to_c]
        if not remote:
            return pltpu.make_async_copy(piece, f_recv.at[z], rz_r)
        return pltpu.make_async_remote_copy(
            piece, f_recv.at[z], rz_s, rz_r,
            device_id=at(x, y, to_h * NZL + core, to_c), device_id_type=MESH,
        )

    for a in (2, 1, 3, 0):
        for b in range(NC):
            if a or b:
                scatter_z(a, b, True).start()

    @pl.when(home)
    def _():
        scatter_z(0, 0, False).start()

    @pl.when(jnp.logical_not(home))
    def _():
        scatter_z(0, 0, True).start()

    pltpu.make_async_copy(zrecv.at[0:7], zrecv.at[0:7], az_s).wait()

    @pl.when(jnp.logical_not(home))
    def _():
        pltpu.make_async_copy(zrecv.at[0], zrecv.at[0], az_s).wait()

    ay_all, ax_all = y_recv.at[0:LAST], x_recv.at[0:LAST]
    pltpu.make_async_copy(ay_all, ay_all, ay_s).wait()
    pltpu.make_async_copy(ax_all, ax_all, ax_s).wait()
    bx_all, by_all = x_recv.at[0, :, 0], c_recv.at[0, :, 0 : NY - 1]
    pltpu.make_async_copy(bx_all, bx_all, bx_s).wait()
    pltpu.make_async_copy(by_all, by_all, by_s).wait()
    pltpu.make_async_copy(c_recv, c_recv, ac_s).wait()
    pltpu.make_async_copy(c_recv, c_recv, rc_s).wait()
    pltpu.make_async_copy(x_recv, x_recv, rx_s).wait()
    pltpu.make_async_copy(y_recv, y_recv, ry_s).wait()
    out.wait()

    pltpu.make_async_copy(f_recv, f_recv, rz_r).wait()
    total = f_recv[0].astype(F32)
    for k in range(1, 8):
        total += f_recv[k].astype(F32)
    gw_ref[...] = total * scale

    pltpu.make_async_copy(f_recv.at[0:7], f_recv.at[0:7], rz_s).wait()

    @pl.when(jnp.logical_not(home))
    def _():
        pltpu.make_async_copy(f_recv.at[0], f_recv.at[0], rz_s).wait()


def on_device(hidden, queries, cotangent, segments, kv_weight):
    any_space = pl.BlockSpec(memory_space=pl.ANY)
    vmem = pl.BlockSpec(memory_space=pltpu.VMEM)
    scale = 1.0 / math.sqrt(lax.axis_size(("dp", "node")) * TOK)
    dma = pltpu.SemaphoreType.DMA
    scratch = [
        ((TOK, 2048), BF16), ((TOK, 1024), BF16), ((TOK, 1024), BF16), ((1, TOK), jnp.int32), ((4, 512), BF16),
        ((16, 128), BF16), ((8, 16, 128), BF16), ((CH, 2, NX, NY, 32, 128), BF16), ((2, 1024, TOK), BF16),
        ((CH, 2, 128, 512), BF16), ((CH, 2, 128, 512), BF16), ((CH, 2, 512, 128), BF16), ((CH, 2, 512, 128), BF16),
        ((128, 128), F32), ((256, 128), F32),
        ((128, 512), F32), ((256, 512), F32), ((128, 512), F32), ((256, 512), F32),
        ((128, 512), BF16), ((256, 512), BF16), ((128, 512), BF16), ((256, 512), BF16), ((CH, TOK, 128), BF16),
        ((CH, NX, NY, 32, 128), BF16), ((CH, NX, NY, 32, 128), BF16),
        ((CH, NX, NY, 32, 128), BF16), ((CH, NX - 1, NY, 32, 128), BF16),
        ((CH, NY, 32, 128), BF16), ((CH, NY - 1, 32, 128), BF16),
        ((CH, 32, 128), BF16), ((8, 16, 128), BF16), ((8, 16, 128), BF16), ((TOK, 2048), BF16),
    ]
    grad_hidden, packed = pl.pallas_call(
        functools.partial(kernel, scale),
        out_shape=(
            jax.ShapeDtypeStruct((TOK, 2048), BF16),
            jax.ShapeDtypeStruct((16, 128), F32),
        ),
        in_specs=[any_space] * 5,
        out_specs=(any_space, vmem),
        scratch_shapes=[pltpu.VMEM(shape, kind) for shape, kind in scratch]
        + [
            dma((5,)), dma,
            dma, dma, dma, dma((LAST, NY - 1)), dma, dma((LAST,)), dma, dma((NX - 1,)), dma, dma, dma, dma((CH,)),
            dma, dma((CH,)), dma, dma((CH, NY)), dma, dma((CH,)), dma, dma,
        ],
        compiler_params=pltpu.CompilerParams(
            collective_id=0, has_side_effects=True, vmem_limit_bytes=62 << 20
        ),
    )(hidden, queries, cotangent, segments, kv_weight)
    grad_weights = packed.reshape(CH, 4, 2, 64).transpose(1, 2, 0, 3).reshape(4, 512)
    return grad_hidden, grad_weights


def solution(mesh):
    placed = P(("dp", "node"), None)
    return jax.shard_map(
        on_device,
        mesh=mesh,
        in_specs=(placed,) * 5,
        out_specs=(placed, placed),
        check_vma=False,
    )
```

```python
import functools
import math

import jax
import jax.numpy as jnp
from jax import lax
from jax.experimental import pallas as pl
from jax.experimental.pallas import tpu as pltpu
from jax.sharding import PartitionSpec as P

HEAD = 64
KV_HEADS = 4
GROUP = 4
TOK = 256
HALF = 128
NX, NY, NZL, NZH, NC = 4, 8, 2, 4, 2
NZC = 16
CH = KV_HEADS
MESH = pl.DeviceIdType.MESH
F32, BF16 = jnp.float32, jnp.bfloat16
NT = (((1,), (1,)), ((), ()))
NEAR = (1, 7, 2, 6, 3, 5, 4)
FAR = (4, 3, 5, 2, 6, 1, 7, 0)
LAST = CH - 1


def dot(a, b):
    return jnp.dot(a, b, preferred_element_type=F32)


def natural(w_ref, j, x):
    both = jnp.stack([w_ref[j, 0, x], w_ref[j, 1, x]], axis=1)
    return both.reshape(512, 128)


def kernel(
    scale,
    hid_hbm, que_hbm, cot_hbm, seg_hbm, kvw_hbm,
    gh_hbm, gw_ref,
    hid, que, cot, seg, kvw,
    blk, zrecv, w, h_t, q_t, c_t, q_n, c_n, bias_a, bias_b,
    s_a, s_b, d_a, d_b, p_a, p_b, ds_a, ds_b, gkv,
    g_send, c_recv, x_send, x_recv, y_send, y_recv, z_sum, z_send, f_recv, gh,
    in_sem, out_sem,
    az_s, az_r, ay_s, ay_r, ax_s, ax_r, bx_s, bx_r, by_s, by_r, ac_s, ac_r,
    rc_s, rc_r, rx_s, rx_r, ry_s, ry_r, rz_s, rz_r,
):
    dp, node = lax.axis_index("dp"), lax.axis_index("node")
    x = dp // (NY * NZL)
    y = (dp // NZL) % NY
    zl = dp % NZL
    zh = node // NC
    core = node % NC
    z = zh * NZL + zl

    def at(x_, y_, z_, c_):
        return ((x_ * NY + y_) * NZL + z_ % NZL, (z_ // NZL) * NC + c_)

    barrier = pltpu.get_barrier_semaphore()

    def greet_z(k):
        other = (z * NC + core + k) % NZC
        pl.semaphore_signal(
            barrier, inc=1, device_id=at(x, y, other // NC, other % NC), device_id_type=MESH
        )

    def greet_y(k):
        pl.semaphore_signal(
            barrier, inc=1, device_id=at(x, (y + k) % NY, z, core), device_id_type=MESH
        )

    def greet_x(k):
        pl.semaphore_signal(
            barrier, inc=1, device_id=at((x + k) % NX, y, z, core), device_id_type=MESH
        )

    for k in (8, 9, 7, 10, 6, 11, 5, 12, 4):
        greet_z(k)
    for k in FAR[:-1]:
        greet_y(k)
    for k in (13, 3, 14, 2, 15, 1):
        greet_z(k)
    for k in (2, 1, 3):
        greet_x(k)

    ins = [
        pltpu.make_async_copy(kvw_hbm, kvw, in_sem.at[0]),
        pltpu.make_async_copy(hid_hbm, hid, in_sem.at[1]),
        pltpu.make_async_copy(que_hbm, que, in_sem.at[2]),
        pltpu.make_async_copy(cot_hbm, cot, in_sem.at[3]),
        pltpu.make_async_copy(seg_hbm, seg, in_sem.at[4]),
    ]
    for cp in ins:
        cp.start()

    ins[0].wait()
    own = kvw[...].astype(F32)
    blk[...] = jnp.concatenate(
        [
            jnp.concatenate([own[:, j * 64 : j * 64 + 64], own[:, 256 + j * 64 : 320 + j * 64]], axis=1)
            for j in range(CH)
        ],
        axis=0,
    ).astype(BF16)
    pl.semaphore_wait(barrier, (NZC - 1) + (NY - 1) + (NX - 1))

    slot = zh * NC + core

    def gather_z(a, b, remote):
        if not remote:
            return pltpu.make_async_copy(blk, zrecv.at[slot], az_r)
        return pltpu.make_async_remote_copy(
            blk, zrecv.at[slot], az_s, az_r,
            device_id=at(x, y, ((zh + a) % NZH) * NZL + (zl + b) % NZL, zl), device_id_type=MESH,
        )

    for a in range(NZH):
        for b in range(NZL):
            if a or b:
                gather_z(a, b, True).start()
    home = core == zl

    @pl.when(home)
    def _():
        gather_z(0, 0, False).start()

    @pl.when(jnp.logical_not(home))
    def _():
        gather_z(0, 0, True).start()

    ins[1].wait()
    for t in range(16):
        cols = hid[:, t * 128 : (t + 1) * 128].astype(F32)
        turned = jnp.transpose(cols).astype(BF16)
        for half in range(4):
            row = t * 2 + half // 2
            h_t[half % 2, row * 32 : row * 32 + 32, :] = turned[half * 32 : half * 32 + 32, :]

    pltpu.make_async_copy(zrecv, zrecv, az_r).wait()
    r_out = lax.broadcasted_iota(jnp.int32, (128, 128), 0)
    r_in = lax.broadcasted_iota(jnp.int32, (128, 128), 1)
    wanted = ((r_out // 4) % 8) * 16 + (r_out // 32) * 4 + r_out % 4
    mine = dot((r_in == wanted).astype(BF16), zrecv[...].reshape(128, 128)).astype(BF16)
    w[:, core, x, y] = mine.reshape(CH, 32, 128)

    def copy_y(j, k):
        return pltpu.make_async_remote_copy(
            w.at[j, core, x, y], w.at[j, core, x, y], ay_s, ay_r.at[j, k - 1],
            device_id=at(x, (y + k) % NY, z, core), device_id_type=MESH,
        )

    def first_x(a):
        return pltpu.make_async_remote_copy(
            w.at[LAST, core, x, y], w.at[LAST, core, x, y], bx_s, bx_r.at[a - 1],
            device_id=at((x + a) % NX, y, z, core), device_id_type=MESH,
        )

    def wait_first_x(a):
        src = (x + NX - a) % NX
        pltpu.make_async_copy(
            w.at[LAST, core, src, y], w.at[LAST, core, src, y], bx_r.at[a - 1]
        ).wait()

    def then_y(xb, k):
        return pltpu.make_async_remote_copy(
            w.at[LAST, core, xb, y], w.at[LAST, core, xb, y], by_s, by_r,
            device_id=at(x, (y + k) % NY, z, core), device_id_type=MESH,
        )

    def wait_y(j, k):
        src = (y + NY - k) % NY
        pltpu.make_async_copy(
            w.at[j, core, x, src], w.at[j, core, x, src], ay_r.at[j, k - 1]
        ).wait()

    def copy_x(j, yb, a):
        return pltpu.make_async_remote_copy(
            w.at[j, core, x, yb], w.at[j, core, x, yb], ax_s, ax_r.at[j],
            device_id=at((x + a) % NX, y, z, core), device_id_type=MESH,
        )

    def send_y(j, carry):
        for k in NEAR:
            copy_y(j, k).start()
        for a in (2, 1, 3):
            copy_x(j, y, a).start()
        return carry

    lax.fori_loop(0, 1, send_y, 0)
    for a in (2, 1, 3):
        first_x(a).start()
    lax.fori_loop(1, LAST, send_y, 0)
    for k in NEAR:
        then_y(x, k).start()

    ins[2].wait()
    ins[3].wait()
    lane = lax.broadcasted_iota(jnp.int32, (TOK, 128), 1)
    low = lane < 64
    zeros = jnp.zeros((64, 512), BF16)
    for j in range(CH):
        for part in range(2):
            q_t[j, part, 64:128, :] = zeros
            c_t[j, part, 0:64, :] = zeros
        for pair in range(2):
            tile = j * 2 + pair
            q = que[:, tile * 128 : (tile + 1) * 128].astype(F32) * 0.125
            c = cot[:, tile * 128 : (tile + 1) * 128].astype(F32)
            q_turn, c_turn = jnp.transpose(q).astype(BF16), jnp.transpose(c).astype(BF16)
            q_swap, c_swap = pltpu.roll(q, 64, 1), pltpu.roll(c, 64, 1)
            q_rows = (jnp.where(low, q, 0.0).astype(BF16), jnp.where(low, q_swap, 0.0).astype(BF16))
            c_rows = (jnp.where(low, 0.0, c_swap).astype(BF16), jnp.where(low, 0.0, c).astype(BF16))
            for side in range(2):
                g = pair * 2 + side
                for part in range(2):
                    toks = slice(part * 128, part * 128 + 128)
                    lanes = slice(g * 128, g * 128 + 128)
                    q_t[j, part, 0:64, lanes] = q_turn[side * 64 : side * 64 + 64, toks]
                    c_t[j, part, 64:128, lanes] = c_turn[side * 64 : side * 64 + 64, toks]
                    q_n[j, part, lanes, :] = q_rows[side][toks, :]
                    c_n[j, part, lanes, :] = c_rows[side][toks, :]

    def forward(j, carry):
        for k in NEAR:
            wait_y(j, k)
            for a in (2, 1, 3):
                copy_x(j, (y + NY - k) % NY, a).start()
        return carry

    lax.fori_loop(0, 1, forward, 0)
    for a in (1, 3, 2):
        wait_first_x(a)
        for k in NEAR:
            then_y((x + NX - a) % NX, k).start()
    lax.fori_loop(1, LAST, forward, 0)

    ins[4].wait()
    seg_i = jnp.broadcast_to(seg[...].astype(F32), (TOK, TOK))
    seg_j = jnp.transpose(seg_i)
    pos_j = lax.broadcasted_iota(jnp.int32, (TOK, TOK), 0)
    pos_i = lax.broadcasted_iota(jnp.int32, (TOK, TOK), 1)
    bias = jnp.where((seg_i == seg_j) & (pos_i >= pos_j), 0.0, -1e30)
    bias_a[...] = bias[0:128, 0:128]
    bias_b[...] = bias[:, 128:256]

    def wait_x(j):
        pltpu.make_async_copy(w.at[j, core, 0:3], w.at[j, core, 0:3], ax_r.at[j]).wait()

    def wait_then_y():
        blocks = w.at[LAST, core, :, 0 : NY - 1]
        pltpu.make_async_copy(blocks, blocks, by_r).wait()

    def other_core():
        return at(x, y, z, 1 - core)

    def copy_core(j):
        return pltpu.make_async_remote_copy(
            w.at[j, core], w.at[j, core], ac_s, ac_r.at[j],
            device_id=other_core(), device_id_type=MESH,
        )

    def wait_core(j):
        pltpu.make_async_copy(w.at[j, 1 - core], w.at[j, 1 - core], ac_r.at[j]).wait()

    wait_x(0)
    copy_core(0).start()

    def heads(s_ref, d_ref, b_ref, p_ref, o_ref):
        for g in range(GROUP):
            lanes = slice(g * 128, g * 128 + 128)
            s = s_ref[:, lanes] + b_ref[...]
            e = jnp.exp(s - jnp.max(s, axis=0, keepdims=True))
            p = e * (1.0 / jnp.sum(e, axis=0, keepdims=True))
            pb = p.astype(BF16)
            d = d_ref[:, lanes]
            delta = jnp.sum(pb.astype(F32) * d, axis=0, keepdims=True)
            p_ref[:, lanes] = pb
            o_ref[:, lanes] = (p * (d - delta)).astype(BF16)

    def copy_rc(j):
        return pltpu.make_async_remote_copy(
            g_send.at[j], c_recv.at[j], rc_s, rc_r.at[j],
            device_id=other_core(), device_id_type=MESH,
        )

    def copy_rx(j, k, a):
        to, yb = (x + a) % NX, (y + k) % NY
        return pltpu.make_async_remote_copy(
            x_send.at[j, to, yb], x_recv.at[j, a - 1, yb], rx_s, rx_r.at[j, k],
            device_id=at(to, y, z, core), device_id_type=MESH,
        )

    def copy_ry(j, k):
        to = (y + k) % NY
        return pltpu.make_async_remote_copy(
            y_send.at[j, to], y_recv.at[j, k - 1], ry_s, ry_r.at[j],
            device_id=at(x, to, z, core), device_id_type=MESH,
        )

    def take_x(j):
        for k in FAR:
            yb = (y + k) % NY
            blocks = x_recv.at[j, :, yb]
            pltpu.make_async_copy(blocks, blocks, rx_r.at[j, k]).wait()
            total = x_send[j, x, yb].astype(F32)
            for a in range(NX - 1):
                total += x_recv[j, a, yb].astype(F32)
            y_send[j, yb] = total.astype(BF16)
            if k:
                copy_ry(j, k).start()

    def take_y(j):
        pltpu.make_async_copy(y_recv.at[j], y_recv.at[j], ry_r.at[j]).wait()
        total = y_send[j, y].astype(F32)
        for k in range(NY - 1):
            total += y_recv[j, k].astype(F32)
        z_sum[j] = total.astype(BF16)

    def both_cores(j):
        pltpu.make_async_copy(c_recv.at[j], c_recv.at[j], rc_r.at[j]).wait()
        part = dot(h_t[core], gkv[j]).reshape(NX, NY, 32, 128) + c_recv[j].astype(F32)
        x_send[j] = part.astype(BF16)
        for k in FAR:
            for a in (2, 1, 3):
                copy_rx(j, k, a).start()

    def chunk(j, carry):
        wait_core(j)
        kv = jnp.zeros((TOK, 128), F32)
        for xx in range(NX):
            kv += dot(hid[:, xx * 512 : (xx + 1) * 512], natural(w, j, xx))
        kv = kv.astype(BF16)
        s_a[...] = dot(kv[0:128], q_t[j, 0])
        d_a[...] = dot(kv[0:128], c_t[j, 0])
        s_b[...] = dot(kv, q_t[j, 1])
        d_b[...] = dot(kv, c_t[j, 1])

        @pl.when(j > 0)
        def _():
            both_cores(j - 1)

        heads(s_a, d_a, bias_a, p_a, ds_a)
        heads(s_b, d_b, bias_b, p_b, ds_b)

        @pl.when(j < LAST - 1)
        def _():
            wait_x(j + 1)
            copy_core(j + 1).start()

        @pl.when(j == LAST - 1)
        def _():
            wait_then_y()
            copy_core(LAST).start()

        late = dot(ds_b[...], q_n[j, 1]) + dot(p_b[...], c_n[j, 1])
        early = dot(ds_a[...], q_n[j, 0]) + dot(p_a[...], c_n[j, 0])
        grad = jnp.concatenate([late[0:128] + early, late[128:256]], axis=0).astype(BF16)
        gkv[j] = grad
        g_send[j] = dot(h_t[1 - core], grad).astype(BF16).reshape(NX, NY, 32, 128)
        copy_rc(j).start()
        return carry

    lax.fori_loop(0, CH, chunk, 0)

    take_x(0)
    both_cores(LAST)
    take_x(1)
    take_x(2)
    grads = jnp.concatenate([gkv[j] for j in range(CH)], axis=1)

    def hidden_part(xx, carry):
        rows = jnp.concatenate([natural(w, j, xx) for j in range(CH)], axis=1)
        cols = pl.ds(pl.multiple_of(xx * 512, 512), 512)
        gh[:, cols] = lax.dot_general(grads, rows, NT, preferred_element_type=F32).astype(BF16)
        return carry

    lax.fori_loop(0, NX, hidden_part, 0)
    out = pltpu.make_async_copy(gh, gh_hbm, out_sem)
    out.start()

    take_x(CH - 1)
    lax.fori_loop(0, CH, lambda j, carry: (take_y(j), carry)[1], 0)

    back = ((r_out % 16) // 4) * 32 + (r_out // 16) * 4 + r_out % 4
    z_send[...] = (
        dot((r_in == back).astype(BF16), z_sum[...].reshape(128, 128)).astype(BF16).reshape(8, 16, 128)
    )

    def scatter_z(a, b, remote):
        to_h, to_c = (zh + a) % NZH, (core + b) % NC
        piece = z_send.at[to_h * NC + to_c]
        if not remote:
            return pltpu.make_async_copy(piece, f_recv.at[z], rz_r)
        return pltpu.make_async_remote_copy(
            piece, f_recv.at[z], rz_s, rz_r,
            device_id=at(x, y, to_h * NZL + core, to_c), device_id_type=MESH,
        )

    for a in (2, 1, 3, 0):
        for b in range(NC):
            if a or b:
                scatter_z(a, b, True).start()

    @pl.when(home)
    def _():
        scatter_z(0, 0, False).start()

    @pl.when(jnp.logical_not(home))
    def _():
        scatter_z(0, 0, True).start()

    pltpu.make_async_copy(zrecv.at[0:7], zrecv.at[0:7], az_s).wait()

    @pl.when(jnp.logical_not(home))
    def _():
        pltpu.make_async_copy(zrecv.at[0], zrecv.at[0], az_s).wait()

    ay_all, ax_all = y_recv.at[0:LAST], x_recv.at[0:LAST]
    pltpu.make_async_copy(ay_all, ay_all, ay_s).wait()
    pltpu.make_async_copy(ax_all, ax_all, ax_s).wait()
    bx_all, by_all = x_recv.at[0, :, 0], c_recv.at[0, :, 0 : NY - 1]
    pltpu.make_async_copy(bx_all, bx_all, bx_s).wait()
    pltpu.make_async_copy(by_all, by_all, by_s).wait()
    pltpu.make_async_copy(c_recv, c_recv, ac_s).wait()
    pltpu.make_async_copy(c_recv, c_recv, rc_s).wait()
    pltpu.make_async_copy(x_recv, x_recv, rx_s).wait()
    pltpu.make_async_copy(y_recv, y_recv, ry_s).wait()

    out.wait()
    pltpu.make_async_copy(f_recv, f_recv, rz_r).wait()
    total = f_recv[0].astype(F32)
    for k in range(1, 8):
        total += f_recv[k].astype(F32)
    total *= scale
    gw_ref[...] = jnp.concatenate(
        [total[4 * j : 4 * j + 4, side * 64 : side * 64 + 64] for side in range(2) for j in range(CH)], axis=1
    )

    pltpu.make_async_copy(f_recv.at[0:7], f_recv.at[0:7], rz_s).wait()

    @pl.when(jnp.logical_not(home))
    def _():
        pltpu.make_async_copy(f_recv.at[0], f_recv.at[0], rz_s).wait()


def on_device(hidden, queries, cotangent, segments, kv_weight):
    hbm = pl.BlockSpec(memory_space=pl.ANY)
    vmem = pl.BlockSpec(memory_space=pltpu.VMEM)
    scale = 1.0 / math.sqrt(lax.axis_size(("dp", "node")) * TOK)
    dma = pltpu.SemaphoreType.DMA
    scratch = [
        ((TOK, 2048), BF16), ((TOK, 1024), BF16), ((TOK, 1024), BF16), ((1, TOK), jnp.int32), ((4, 512), BF16),
        ((16, 128), BF16), ((8, 16, 128), BF16), ((CH, 2, NX, NY, 32, 128), BF16), ((2, 1024, TOK), BF16),
        ((CH, 2, 128, 512), BF16), ((CH, 2, 128, 512), BF16), ((CH, 2, 512, 128), BF16), ((CH, 2, 512, 128), BF16),
        ((128, 128), F32), ((256, 128), F32),
        ((128, 512), F32), ((256, 512), F32), ((128, 512), F32), ((256, 512), F32),
        ((128, 512), BF16), ((256, 512), BF16), ((128, 512), BF16), ((256, 512), BF16), ((CH, TOK, 128), BF16),
        ((CH, NX, NY, 32, 128), BF16), ((CH, NX, NY, 32, 128), BF16),
        ((CH, NX, NY, 32, 128), BF16), ((CH, NX - 1, NY, 32, 128), BF16),
        ((CH, NY, 32, 128), BF16), ((CH, NY - 1, 32, 128), BF16),
        ((CH, 32, 128), BF16), ((8, 16, 128), BF16), ((8, 16, 128), BF16), ((TOK, 2048), BF16),
    ]
    return pl.pallas_call(
        functools.partial(kernel, scale),
        out_shape=(
            jax.ShapeDtypeStruct((TOK, 2048), BF16),
            jax.ShapeDtypeStruct((4, 512), F32),
        ),
        in_specs=[hbm] * 5,
        out_specs=(hbm, vmem),
        scratch_shapes=[pltpu.VMEM(shape, kind) for shape, kind in scratch]
        + [
            dma((5,)), dma,
            dma, dma, dma, dma((LAST, NY - 1)), dma, dma((LAST,)), dma, dma((NX - 1,)), dma, dma, dma, dma((CH,)),
            dma, dma((CH,)), dma, dma((CH, NY)), dma, dma((CH,)), dma, dma,
        ],
        compiler_params=pltpu.CompilerParams(
            collective_id=0, has_side_effects=True, vmem_limit_bytes=62 << 20
        ),
    )(hidden, queries, cotangent, segments, kv_weight)


def solution(mesh):
    placed = P(("dp", "node"), None)
    return jax.shard_map(
        on_device,
        mesh=mesh,
        in_specs=(placed,) * 5,
        out_specs=(placed, placed),
        check_vma=False,
    )
```

```python
import functools
import math

import jax
import jax.numpy as jnp
from jax import lax
from jax.experimental import pallas as pl
from jax.experimental.pallas import tpu as pltpu
from jax.sharding import PartitionSpec as P

HEAD = 64
KV_HEADS = 4
GROUP = 4
TOK = 256
HALF = 128
NX, NY, NZL, NZH, NC = 4, 8, 2, 4, 2
NZC = 16
CH = KV_HEADS
MESH = pl.DeviceIdType.MESH
F32, BF16 = jnp.float32, jnp.bfloat16
NT = (((1,), (1,)), ((), ()))
NEAR = (1, 7, 2, 6, 3, 5, 4)
FAR = (4, 3, 5, 2, 6, 1, 7, 0)
LAST = CH - 1


def dot(a, b):
    return jnp.dot(a, b, preferred_element_type=F32)


def natural(w_ref, j, x):
    both = jnp.stack([w_ref[j, 0, x], w_ref[j, 1, x]], axis=1)
    return both.reshape(512, 128)


def kernel(
    scale,
    hid_hbm, que_hbm, cot_hbm, seg_hbm, kvw_hbm,
    gh_hbm, gw_ref,
    hid, que, cot, seg, kvw,
    blk, zrecv, w, h_t, q_t, c_t, q_n, c_n, bias_a, bias_b,
    s_a, s_b, d_a, d_b, p_a, p_b, ds_a, ds_b, gkv,
    g_send, c_recv, x_send, x_recv, y_send, y_recv, z_sum, z_send, f_recv, gh,
    in_sem, out_sem,
    az_s, az_r, ay_s, ay_r, ax_s, ax_r, bx_s, bx_r, by_s, by_r, ac_s, ac_r,
    rc_s, rc_r, rx_s, rx_r, ry_s, ry_r, rz_s, rz_r,
):
    dp, node = lax.axis_index("dp"), lax.axis_index("node")
    x = dp // (NY * NZL)
    y = (dp // NZL) % NY
    zl = dp % NZL
    zh = node // NC
    core = node % NC
    z = zh * NZL + zl

    def at(x_, y_, z_, c_):
        return ((x_ * NY + y_) * NZL + z_ % NZL, (z_ // NZL) * NC + c_)

    barrier = pltpu.get_barrier_semaphore()

    def greet_z(k):
        other = (z * NC + core + k) % NZC
        pl.semaphore_signal(
            barrier, inc=1, device_id=at(x, y, other // NC, other % NC), device_id_type=MESH
        )

    def greet_y(k):
        pl.semaphore_signal(
            barrier, inc=1, device_id=at(x, (y + k) % NY, z, core), device_id_type=MESH
        )

    def greet_x(k):
        pl.semaphore_signal(
            barrier, inc=1, device_id=at((x + k) % NX, y, z, core), device_id_type=MESH
        )

    for k in (8, 9, 7, 10, 6, 11, 5, 12, 4):
        greet_z(k)
    for k in FAR[:-1]:
        greet_y(k)
    for k in (13, 3, 14, 2, 15, 1):
        greet_z(k)
    for k in (2, 1, 3):
        greet_x(k)

    ins = [
        pltpu.make_async_copy(kvw_hbm, kvw, in_sem.at[0]),
        pltpu.make_async_copy(hid_hbm, hid, in_sem.at[1]),
        pltpu.make_async_copy(que_hbm, que, in_sem.at[2]),
        pltpu.make_async_copy(cot_hbm, cot, in_sem.at[3]),
        pltpu.make_async_copy(seg_hbm, seg, in_sem.at[4]),
    ]
    for cp in ins:
        cp.start()

    ins[0].wait()
    own = kvw[...].astype(F32)
    blk[...] = jnp.concatenate(
        [
            jnp.concatenate([own[:, j * 64 : j * 64 + 64], own[:, 256 + j * 64 : 320 + j * 64]], axis=1)
            for j in range(CH)
        ],
        axis=0,
    ).astype(BF16)
    pl.semaphore_wait(barrier, (NZC - 1) + (NY - 1) + (NX - 1))

    slot = zh * NC + core

    def gather_z(a, b, remote):
        if not remote:
            return pltpu.make_async_copy(blk, zrecv.at[slot], az_r)
        return pltpu.make_async_remote_copy(
            blk, zrecv.at[slot], az_s, az_r,
            device_id=at(x, y, ((zh + a) % NZH) * NZL + (zl + b) % NZL, zl), device_id_type=MESH,
        )

    for a in range(NZH):
        for b in range(NZL):
            if a or b:
                gather_z(a, b, True).start()
    home = core == zl

    @pl.when(home)
    def _():
        gather_z(0, 0, False).start()

    @pl.when(jnp.logical_not(home))
    def _():
        gather_z(0, 0, True).start()

    ins[1].wait()
    for t in range(16):
        cols = hid[:, t * 128 : (t + 1) * 128].astype(F32)
        turned = jnp.transpose(cols).astype(BF16)
        for half in range(4):
            row = t * 2 + half // 2
            h_t[half % 2, row * 32 : row * 32 + 32, :] = turned[half * 32 : half * 32 + 32, :]

    pltpu.make_async_copy(zrecv, zrecv, az_r).wait()
    r_out = lax.broadcasted_iota(jnp.int32, (128, 128), 0)
    r_in = lax.broadcasted_iota(jnp.int32, (128, 128), 1)
    wanted = ((r_out // 4) % 8) * 16 + (r_out // 32) * 4 + r_out % 4
    mine = dot((r_in == wanted).astype(BF16), zrecv[...].reshape(128, 128)).astype(BF16)
    w[:, core, x, y] = mine.reshape(CH, 32, 128)

    def copy_y(j, k):
        return pltpu.make_async_remote_copy(
            w.at[j, core, x, y], w.at[j, core, x, y], ay_s, ay_r.at[j, k - 1],
            device_id=at(x, (y + k) % NY, z, core), device_id_type=MESH,
        )

    def first_x(a):
        return pltpu.make_async_remote_copy(
            w.at[LAST, core, x, y], w.at[LAST, core, x, y], bx_s, bx_r.at[a - 1],
            device_id=at((x + a) % NX, y, z, core), device_id_type=MESH,
        )

    def wait_first_x(a):
        src = (x + NX - a) % NX
        pltpu.make_async_copy(
            w.at[LAST, core, src, y], w.at[LAST, core, src, y], bx_r.at[a - 1]
        ).wait()

    def then_y(xb, k):
        return pltpu.make_async_remote_copy(
            w.at[LAST, core, xb, y], w.at[LAST, core, xb, y], by_s, by_r,
            device_id=at(x, (y + k) % NY, z, core), device_id_type=MESH,
        )

    def wait_y(j, k):
        src = (y + NY - k) % NY
        pltpu.make_async_copy(
            w.at[j, core, x, src], w.at[j, core, x, src], ay_r.at[j, k - 1]
        ).wait()

    def copy_x(j, yb, a):
        return pltpu.make_async_remote_copy(
            w.at[j, core, x, yb], w.at[j, core, x, yb], ax_s, ax_r.at[j],
            device_id=at((x + a) % NX, y, z, core), device_id_type=MESH,
        )

    def send_y(j, carry):
        for k in NEAR:
            copy_y(j, k).start()
        for a in (2, 1, 3):
            copy_x(j, y, a).start()
        return carry

    lax.fori_loop(0, 1, send_y, 0)
    for a in (2, 1, 3):
        first_x(a).start()
    lax.fori_loop(1, LAST, send_y, 0)
    for k in NEAR:
        then_y(x, k).start()

    ins[2].wait()
    ins[3].wait()
    lane = lax.broadcasted_iota(jnp.int32, (TOK, 128), 1)
    low = lane < 64
    zeros = jnp.zeros((64, 512), BF16)
    for j in range(CH):
        for part in range(2):
            q_t[j, part, 64:128, :] = zeros
            c_t[j, part, 0:64, :] = zeros
        for pair in range(2):
            tile = j * 2 + pair
            q = que[:, tile * 128 : (tile + 1) * 128].astype(F32) * 0.125
            c = cot[:, tile * 128 : (tile + 1) * 128].astype(F32)
            q_turn, c_turn = jnp.transpose(q).astype(BF16), jnp.transpose(c).astype(BF16)
            q_swap, c_swap = pltpu.roll(q, 64, 1), pltpu.roll(c, 64, 1)
            q_rows = (jnp.where(low, q, 0.0).astype(BF16), jnp.where(low, q_swap, 0.0).astype(BF16))
            c_rows = (jnp.where(low, 0.0, c_swap).astype(BF16), jnp.where(low, 0.0, c).astype(BF16))
            for side in range(2):
                g = pair * 2 + side
                for part in range(2):
                    toks = slice(part * 128, part * 128 + 128)
                    lanes = slice(g * 128, g * 128 + 128)
                    q_t[j, part, 0:64, lanes] = q_turn[side * 64 : side * 64 + 64, toks]
                    c_t[j, part, 64:128, lanes] = c_turn[side * 64 : side * 64 + 64, toks]
                    q_n[j, part, lanes, :] = q_rows[side][toks, :]
                    c_n[j, part, lanes, :] = c_rows[side][toks, :]

    def forward(j, carry):
        for k in NEAR:
            wait_y(j, k)
            for a in (2, 1, 3):
                copy_x(j, (y + NY - k) % NY, a).start()
        return carry

    lax.fori_loop(0, 1, forward, 0)
    for a in (1, 3, 2):
        wait_first_x(a)
        for k in NEAR:
            then_y((x + NX - a) % NX, k).start()
    lax.fori_loop(1, LAST, forward, 0)

    ins[4].wait()
    seg_i = jnp.broadcast_to(seg[...].astype(F32), (TOK, TOK))
    seg_j = jnp.transpose(seg_i)
    pos_j = lax.broadcasted_iota(jnp.int32, (TOK, TOK), 0)
    pos_i = lax.broadcasted_iota(jnp.int32, (TOK, TOK), 1)
    bias = jnp.where((seg_i == seg_j) & (pos_i >= pos_j), 0.0, -1e30)
    bias_a[...] = bias[0:128, 0:128]
    bias_b[...] = bias[:, 128:256]

    def wait_x(j):
        pltpu.make_async_copy(w.at[j, core, 0:3], w.at[j, core, 0:3], ax_r.at[j]).wait()

    def wait_then_y():
        blocks = w.at[LAST, core, :, 0 : NY - 1]
        pltpu.make_async_copy(blocks, blocks, by_r).wait()

    def other_core():
        return at(x, y, z, 1 - core)

    def copy_core(j):
        return pltpu.make_async_remote_copy(
            w.at[j, core], w.at[j, core], ac_s, ac_r.at[j],
            device_id=other_core(), device_id_type=MESH,
        )

    def wait_core(j):
        pltpu.make_async_copy(w.at[j, 1 - core], w.at[j, 1 - core], ac_r.at[j]).wait()

    wait_x(0)
    copy_core(0).start()

    def heads(s_ref, d_ref, b_ref, p_ref, o_ref):
        for g in range(GROUP):
            lanes = slice(g * 128, g * 128 + 128)
            s = s_ref[:, lanes] + b_ref[...]
            e = jnp.exp(s - jnp.max(s, axis=0, keepdims=True))
            p = e * (1.0 / jnp.sum(e, axis=0, keepdims=True))
            pb = p.astype(BF16)
            d = d_ref[:, lanes]
            delta = jnp.sum(pb.astype(F32) * d, axis=0, keepdims=True)
            p_ref[:, lanes] = pb
            o_ref[:, lanes] = (p * (d - delta)).astype(BF16)

    def copy_rc(j):
        return pltpu.make_async_remote_copy(
            g_send.at[j], c_recv.at[j], rc_s, rc_r.at[j],
            device_id=other_core(), device_id_type=MESH,
        )

    def copy_rx(j, k, a):
        to, yb = (x + a) % NX, (y + k) % NY
        return pltpu.make_async_remote_copy(
            x_send.at[j, to, yb], x_recv.at[j, a - 1, yb], rx_s, rx_r.at[j, k],
            device_id=at(to, y, z, core), device_id_type=MESH,
        )

    def copy_ry(j, k):
        to = (y + k) % NY
        return pltpu.make_async_remote_copy(
            y_send.at[j, to], y_recv.at[j, k - 1], ry_s, ry_r.at[j],
            device_id=at(x, to, z, core), device_id_type=MESH,
        )

    def take_x(j):
        for k in FAR:
            yb = (y + k) % NY
            blocks = x_recv.at[j, :, yb]
            pltpu.make_async_copy(blocks, blocks, rx_r.at[j, k]).wait()
            total = x_send[j, x, yb].astype(F32)
            for a in range(NX - 1):
                total += x_recv[j, a, yb].astype(F32)
            y_send[j, yb] = total.astype(BF16)
            if k:
                copy_ry(j, k).start()

    def take_y(j):
        pltpu.make_async_copy(y_recv.at[j], y_recv.at[j], ry_r.at[j]).wait()
        total = y_send[j, y].astype(F32)
        for k in range(NY - 1):
            total += y_recv[j, k].astype(F32)
        z_sum[j] = total.astype(BF16)

    def both_cores(j):
        pltpu.make_async_copy(c_recv.at[j], c_recv.at[j], rc_r.at[j]).wait()
        part = dot(h_t[core], gkv[j]).reshape(NX, NY, 32, 128) + c_recv[j].astype(F32)
        x_send[j] = part.astype(BF16)
        for k in FAR:
            for a in (2, 1, 3):
                copy_rx(j, k, a).start()

    def chunk(j, carry):
        wait_core(j)
        kv = jnp.zeros((TOK, 128), F32)
        for xx in range(NX):
            kv += dot(hid[:, xx * 512 : (xx + 1) * 512], natural(w, j, xx))
        kv = kv.astype(BF16)
        s_a[...] = dot(kv[0:128], q_t[j, 0])
        d_a[...] = dot(kv[0:128], c_t[j, 0])
        s_b[...] = dot(kv, q_t[j, 1])
        d_b[...] = dot(kv, c_t[j, 1])

        @pl.when(j > 0)
        def _():
            both_cores(j - 1)

        heads(s_a, d_a, bias_a, p_a, ds_a)
        heads(s_b, d_b, bias_b, p_b, ds_b)

        @pl.when(j < LAST - 1)
        def _():
            wait_x(j + 1)
            copy_core(j + 1).start()

        @pl.when(j == LAST - 1)
        def _():
            wait_then_y()
            copy_core(LAST).start()

        late = dot(ds_b[...], q_n[j, 1]) + dot(p_b[...], c_n[j, 1])
        early = dot(ds_a[...], q_n[j, 0]) + dot(p_a[...], c_n[j, 0])
        grad = jnp.concatenate([late[0:128] + early, late[128:256]], axis=0).astype(BF16)
        gkv[j] = grad
        g_send[j] = dot(h_t[1 - core], grad).astype(BF16).reshape(NX, NY, 32, 128)
        copy_rc(j).start()
        return carry

    lax.fori_loop(0, CH, chunk, 0)

    take_x(0)
    both_cores(LAST)
    take_x(1)
    take_x(2)
    grads = jnp.concatenate([gkv[j] for j in range(CH)], axis=1)

    def hidden_part(xx, carry):
        rows = jnp.concatenate([natural(w, j, xx) for j in range(CH)], axis=1)
        cols = pl.ds(pl.multiple_of(xx * 512, 512), 512)
        gh[:, cols] = lax.dot_general(grads, rows, NT, preferred_element_type=F32).astype(BF16)
        return carry

    lax.fori_loop(0, NX, hidden_part, 0)
    out = pltpu.make_async_copy(gh, gh_hbm, out_sem)
    out.start()

    take_x(CH - 1)
    lax.fori_loop(0, CH, lambda j, carry: (take_y(j), carry)[1], 0)

    back = ((r_out % 16) // 4) * 32 + (r_out // 16) * 4 + r_out % 4
    z_send[...] = (
        dot((r_in == back).astype(BF16), z_sum[...].reshape(128, 128)).astype(BF16).reshape(8, 16, 128)
    )

    def scatter_z(a, b, remote):
        to_h, to_c = (zh + a) % NZH, (core + b) % NC
        piece = z_send.at[to_h * NC + to_c]
        if not remote:
            return pltpu.make_async_copy(piece, f_recv.at[z], rz_r)
        return pltpu.make_async_remote_copy(
            piece, f_recv.at[z], rz_s, rz_r,
            device_id=at(x, y, to_h * NZL + core, to_c), device_id_type=MESH,
        )

    for a in (2, 1, 3, 0):
        for b in range(NC):
            if a or b:
                scatter_z(a, b, True).start()

    @pl.when(home)
    def _():
        scatter_z(0, 0, False).start()

    @pl.when(jnp.logical_not(home))
    def _():
        scatter_z(0, 0, True).start()

    pltpu.make_async_copy(zrecv.at[0:7], zrecv.at[0:7], az_s).wait()

    @pl.when(jnp.logical_not(home))
    def _():
        pltpu.make_async_copy(zrecv.at[0], zrecv.at[0], az_s).wait()

    ay_all, ax_all = y_recv.at[0:LAST], x_recv.at[0:LAST]
    pltpu.make_async_copy(ay_all, ay_all, ay_s).wait()
    pltpu.make_async_copy(ax_all, ax_all, ax_s).wait()
    bx_all, by_all = x_recv.at[0, :, 0], c_recv.at[0, :, 0 : NY - 1]
    pltpu.make_async_copy(bx_all, bx_all, bx_s).wait()
    pltpu.make_async_copy(by_all, by_all, by_s).wait()
    pltpu.make_async_copy(c_recv, c_recv, ac_s).wait()
    pltpu.make_async_copy(c_recv, c_recv, rc_s).wait()
    pltpu.make_async_copy(x_recv, x_recv, rx_s).wait()
    pltpu.make_async_copy(y_recv, y_recv, ry_s).wait()

    out.wait()
    pltpu.make_async_copy(f_recv, f_recv, rz_r).wait()
    total = f_recv[0].astype(F32)
    for k in range(1, 8):
        total += f_recv[k].astype(F32)
    total *= scale
    gw_ref[...] = jnp.concatenate(
        [total[4 * j : 4 * j + 4, side * 64 : side * 64 + 64] for side in range(2) for j in range(CH)], axis=1
    )

    pltpu.make_async_copy(f_recv.at[0:7], f_recv.at[0:7], rz_s).wait()

    @pl.when(jnp.logical_not(home))
    def _():
        pltpu.make_async_copy(f_recv.at[0], f_recv.at[0], rz_s).wait()


def on_device(hidden, queries, cotangent, segments, kv_weight):
    hbm = pl.BlockSpec(memory_space=pl.ANY)
    vmem = pl.BlockSpec(memory_space=pltpu.VMEM)
    scale = 1.0 / math.sqrt(lax.axis_size(("dp", "node")) * TOK)
    dma = pltpu.SemaphoreType.DMA
    scratch = [
        ((TOK, 2048), BF16), ((TOK, 1024), BF16), ((TOK, 1024), BF16), ((1, TOK), jnp.int32), ((4, 512), BF16),
        ((16, 128), BF16), ((8, 16, 128), BF16), ((CH, 2, NX, NY, 32, 128), BF16), ((2, 1024, TOK), BF16),
        ((CH, 2, 128, 512), BF16), ((CH, 2, 128, 512), BF16), ((CH, 2, 512, 128), BF16), ((CH, 2, 512, 128), BF16),
        ((128, 128), F32), ((256, 128), F32),
        ((128, 512), F32), ((256, 512), F32), ((128, 512), F32), ((256, 512), F32),
        ((128, 512), BF16), ((256, 512), BF16), ((128, 512), BF16), ((256, 512), BF16), ((CH, TOK, 128), BF16),
        ((CH, NX, NY, 32, 128), BF16), ((CH, NX, NY, 32, 128), BF16),
        ((CH, NX, NY, 32, 128), BF16), ((CH, NX - 1, NY, 32, 128), BF16),
        ((CH, NY, 32, 128), BF16), ((CH, NY - 1, 32, 128), BF16),
        ((CH, 32, 128), BF16), ((8, 16, 128), BF16), ((8, 16, 128), BF16), ((TOK, 2048), BF16),
    ]
    return pl.pallas_call(
        functools.partial(kernel, scale),
        out_shape=(
            jax.ShapeDtypeStruct((TOK, 2048), BF16),
            jax.ShapeDtypeStruct((4, 512), F32),
        ),
        in_specs=[hbm] * 5,
        out_specs=(hbm, vmem),
        scratch_shapes=[pltpu.VMEM(shape, kind) for shape, kind in scratch]
        + [
            dma((5,)), dma,
            dma, dma, dma, dma((LAST, NY - 1)), dma, dma((LAST,)), dma, dma((NX - 1,)), dma, dma, dma, dma((CH,)),
            dma, dma((CH,)), dma, dma((CH, NY)), dma, dma((CH,)), dma, dma,
        ],
        compiler_params=pltpu.CompilerParams(
            collective_id=0, has_side_effects=True, vmem_limit_bytes=40 << 20
        ),
    )(
        *(
            pltpu.with_memory_space_constraint(array, pltpu.HBM)
            for array in (hidden, queries, cotangent, segments, kv_weight)
        )
    )


def solution(mesh):
    placed = P(("dp", "node"), None)
    return jax.shard_map(
        on_device,
        mesh=mesh,
        in_specs=(placed,) * 5,
        out_specs=(placed, placed),
        check_vma=False,
    )
```

```python
import functools
import math

import jax
import jax.numpy as jnp
from jax import lax
from jax.experimental import pallas as pl
from jax.experimental.pallas import tpu as pltpu
from jax.sharding import PartitionSpec as P

HEAD = 64
KV_HEADS = 4
GROUP = 4
TOK = 256
HALF = 128
NX, NY, NZL, NZH, NC = 4, 8, 2, 4, 2
NZC = 16
CH = KV_HEADS
MESH = pl.DeviceIdType.MESH
F32, BF16 = jnp.float32, jnp.bfloat16
NT = (((1,), (1,)), ((), ()))
NEAR = (1, 7, 2, 6, 3, 5, 4)
FAR = (4, 3, 5, 2, 6, 1, 7, 0)
LAST = CH - 1


def dot(a, b):
    return jnp.dot(a, b, preferred_element_type=F32)


def natural(w_ref, j, x):
    both = jnp.stack([w_ref[j, 0, x], w_ref[j, 1, x]], axis=1)
    return both.reshape(512, 128)


def kernel(
    scale,
    hid_hbm, que_hbm, cot_hbm, seg_hbm, kvw_hbm,
    gh_hbm, gw_ref,
    hid, que, cot, seg, kvw,
    blk, zrecv, w, h_t, q_t, c_t, q_n, c_n, bias_a, bias_b,
    s_a, s_b, d_a, d_b, p_a, p_b, ds_a, ds_b, gkv,
    g_send, c_recv, x_send, x_recv, y_send, y_recv, z_sum, z_send, f_recv, gh,
    in_sem, out_sem,
    az_s, az_r, ay_s, ay_r, ax_s, ax_r, bx_s, bx_r, by_s, by_r, ac_s, ac_r,
    rc_s, rc_r, rx_s, rx_r, ry_s, ry_r, rz_s, rz_r,
):
    dp, node = lax.axis_index("dp"), lax.axis_index("node")
    x = dp // (NY * NZL)
    y = (dp // NZL) % NY
    zl = dp % NZL
    zh = node // NC
    core = node % NC
    z = zh * NZL + zl

    def at(x_, y_, z_, c_):
        return ((x_ * NY + y_) * NZL + z_ % NZL, (z_ // NZL) * NC + c_)

    ins = [
        pltpu.make_async_copy(kvw_hbm, kvw, in_sem.at[0]),
        pltpu.make_async_copy(hid_hbm, hid, in_sem.at[1]),
        pltpu.make_async_copy(que_hbm, que, in_sem.at[2]),
        pltpu.make_async_copy(cot_hbm, cot, in_sem.at[3]),
        pltpu.make_async_copy(seg_hbm, seg, in_sem.at[4]),
    ]
    ins[0].start()

    barrier = pltpu.get_barrier_semaphore()

    def greet_z(k):
        other = (z * NC + core + k) % NZC
        pl.semaphore_signal(
            barrier, inc=1, device_id=at(x, y, other // NC, other % NC), device_id_type=MESH
        )

    def greet_y(k):
        pl.semaphore_signal(
            barrier, inc=1, device_id=at(x, (y + k) % NY, z, core), device_id_type=MESH
        )

    def greet_x(k):
        pl.semaphore_signal(
            barrier, inc=1, device_id=at((x + k) % NX, y, z, core), device_id_type=MESH
        )

    for k in (8, 9, 7, 10, 6, 11, 5, 12, 4):
        greet_z(k)
    for k in FAR[:-1]:
        greet_y(k)
    for k in (13, 3, 14, 2, 15, 1):
        greet_z(k)
    for k in (2, 1, 3):
        greet_x(k)

    for cp in ins[1:]:
        cp.start()

    ins[0].wait()
    own = kvw[...].astype(F32)
    blk[...] = jnp.concatenate(
        [
            jnp.concatenate([own[:, j * 64 : j * 64 + 64], own[:, 256 + j * 64 : 320 + j * 64]], axis=1)
            for j in range(CH)
        ],
        axis=0,
    ).astype(BF16)
    pl.semaphore_wait(barrier, (NZC - 1) + (NY - 1) + (NX - 1))

    slot = zh * NC + core

    def gather_z(a, b, remote):
        if not remote:
            return pltpu.make_async_copy(blk, zrecv.at[slot], az_r)
        return pltpu.make_async_remote_copy(
            blk, zrecv.at[slot], az_s, az_r,
            device_id=at(x, y, ((zh + a) % NZH) * NZL + (zl + b) % NZL, zl), device_id_type=MESH,
        )

    for a in range(NZH):
        for b in range(NZL):
            if a or b:
                gather_z(a, b, True).start()
    home = core == zl

    @pl.when(home)
    def _():
        gather_z(0, 0, False).start()

    @pl.when(jnp.logical_not(home))
    def _():
        gather_z(0, 0, True).start()

    ins[1].wait()
    for t in range(16):
        cols = hid[:, t * 128 : (t + 1) * 128].astype(F32)
        turned = jnp.transpose(cols).astype(BF16)
        for half in range(4):
            row = t * 2 + half // 2
            h_t[half % 2, row * 32 : row * 32 + 32, :] = turned[half * 32 : half * 32 + 32, :]

    pltpu.make_async_copy(zrecv, zrecv, az_r).wait()
    r_out = lax.broadcasted_iota(jnp.int32, (128, 128), 0)
    r_in = lax.broadcasted_iota(jnp.int32, (128, 128), 1)
    wanted = ((r_out // 4) % 8) * 16 + (r_out // 32) * 4 + r_out % 4
    mine = dot((r_in == wanted).astype(BF16), zrecv[...].reshape(128, 128)).astype(BF16)
    w[:, core, x, y] = mine.reshape(CH, 32, 128)

    def copy_y(j, k):
        return pltpu.make_async_remote_copy(
            w.at[j, core, x, y], w.at[j, core, x, y], ay_s, ay_r.at[j, k - 1],
            device_id=at(x, (y + k) % NY, z, core), device_id_type=MESH,
        )

    def first_x(a):
        return pltpu.make_async_remote_copy(
            w.at[LAST, core, x, y], w.at[LAST, core, x, y], bx_s, bx_r.at[a - 1],
            device_id=at((x + a) % NX, y, z, core), device_id_type=MESH,
        )

    def wait_first_x(a):
        src = (x + NX - a) % NX
        pltpu.make_async_copy(
            w.at[LAST, core, src, y], w.at[LAST, core, src, y], bx_r.at[a - 1]
        ).wait()

    def then_y(xb, k):
        return pltpu.make_async_remote_copy(
            w.at[LAST, core, xb, y], w.at[LAST, core, xb, y], by_s, by_r,
            device_id=at(x, (y + k) % NY, z, core), device_id_type=MESH,
        )

    def wait_y(j, k):
        src = (y + NY - k) % NY
        pltpu.make_async_copy(
            w.at[j, core, x, src], w.at[j, core, x, src], ay_r.at[j, k - 1]
        ).wait()

    def copy_x(j, yb, a):
        return pltpu.make_async_remote_copy(
            w.at[j, core, x, yb], w.at[j, core, x, yb], ax_s, ax_r.at[j],
            device_id=at((x + a) % NX, y, z, core), device_id_type=MESH,
        )

    def send_y(j, carry):
        for k in NEAR:
            copy_y(j, k).start()
        for a in (2, 1, 3):
            copy_x(j, y, a).start()
        return carry

    lax.fori_loop(0, 1, send_y, 0)
    for a in (2, 1, 3):
        first_x(a).start()
    lax.fori_loop(1, LAST, send_y, 0)
    for k in NEAR:
        then_y(x, k).start()

    ins[2].wait()
    ins[3].wait()
    lane = lax.broadcasted_iota(jnp.int32, (TOK, 128), 1)
    low = lane < 64
    zeros = jnp.zeros((64, 512), BF16)
    for j in range(CH):
        for part in range(2):
            q_t[j, part, 64:128, :] = zeros
            c_t[j, part, 0:64, :] = zeros
        for pair in range(2):
            tile = j * 2 + pair
            q = que[:, tile * 128 : (tile + 1) * 128].astype(F32) * 0.125
            c = cot[:, tile * 128 : (tile + 1) * 128].astype(F32)
            q_turn, c_turn = jnp.transpose(q).astype(BF16), jnp.transpose(c).astype(BF16)
            q_swap, c_swap = pltpu.roll(q, 64, 1), pltpu.roll(c, 64, 1)
            q_rows = (jnp.where(low, q, 0.0).astype(BF16), jnp.where(low, q_swap, 0.0).astype(BF16))
            c_rows = (jnp.where(low, 0.0, c_swap).astype(BF16), jnp.where(low, 0.0, c).astype(BF16))
            for side in range(2):
                g = pair * 2 + side
                for part in range(2):
                    toks = slice(part * 128, part * 128 + 128)
                    lanes = slice(g * 128, g * 128 + 128)
                    q_t[j, part, 0:64, lanes] = q_turn[side * 64 : side * 64 + 64, toks]
                    c_t[j, part, 64:128, lanes] = c_turn[side * 64 : side * 64 + 64, toks]
                    q_n[j, part, lanes, :] = q_rows[side][toks, :]
                    c_n[j, part, lanes, :] = c_rows[side][toks, :]

    def forward(j, carry):
        for k in NEAR:
            wait_y(j, k)
            for a in (2, 1, 3):
                copy_x(j, (y + NY - k) % NY, a).start()
        return carry

    lax.fori_loop(0, 1, forward, 0)
    for a in (1, 3, 2):
        wait_first_x(a)
        for k in NEAR:
            then_y((x + NX - a) % NX, k).start()
    lax.fori_loop(1, LAST, forward, 0)

    ins[4].wait()
    seg_i = jnp.broadcast_to(seg[...].astype(F32), (TOK, TOK))
    seg_j = jnp.transpose(seg_i)
    pos_j = lax.broadcasted_iota(jnp.int32, (TOK, TOK), 0)
    pos_i = lax.broadcasted_iota(jnp.int32, (TOK, TOK), 1)
    bias = jnp.where((seg_i == seg_j) & (pos_i >= pos_j), 0.0, -1e30)
    bias_a[...] = bias[0:128, 0:128]
    bias_b[...] = bias[:, 128:256]

    def wait_x(j):
        pltpu.make_async_copy(w.at[j, core, 0:3], w.at[j, core, 0:3], ax_r.at[j]).wait()

    def wait_then_y():
        blocks = w.at[LAST, core, :, 0 : NY - 1]
        pltpu.make_async_copy(blocks, blocks, by_r).wait()

    def other_core():
        return at(x, y, z, 1 - core)

    def copy_core(j):
        return pltpu.make_async_remote_copy(
            w.at[j, core], w.at[j, core], ac_s, ac_r.at[j],
            device_id=other_core(), device_id_type=MESH,
        )

    def wait_core(j):
        pltpu.make_async_copy(w.at[j, 1 - core], w.at[j, 1 - core], ac_r.at[j]).wait()

    wait_x(0)
    copy_core(0).start()

    def heads(s_ref, d_ref, b_ref, p_ref, o_ref):
        for g in range(GROUP):
            lanes = slice(g * 128, g * 128 + 128)
            s = s_ref[:, lanes] + b_ref[...]
            e = jnp.exp(s - jnp.max(s, axis=0, keepdims=True))
            p = e * (1.0 / jnp.sum(e, axis=0, keepdims=True))
            pb = p.astype(BF16)
            d = d_ref[:, lanes]
            delta = jnp.sum(pb.astype(F32) * d, axis=0, keepdims=True)
            p_ref[:, lanes] = pb
            o_ref[:, lanes] = (p * (d - delta)).astype(BF16)

    def copy_rc(j):
        return pltpu.make_async_remote_copy(
            g_send.at[j], c_recv.at[j], rc_s, rc_r.at[j],
            device_id=other_core(), device_id_type=MESH,
        )

    def copy_rx(j, k, a):
        to, yb = (x + a) % NX, (y + k) % NY
        return pltpu.make_async_remote_copy(
            x_send.at[j, to, yb], x_recv.at[j, a - 1, yb], rx_s, rx_r.at[j, k],
            device_id=at(to, y, z, core), device_id_type=MESH,
        )

    def copy_ry(j, k):
        to = (y + k) % NY
        return pltpu.make_async_remote_copy(
            y_send.at[j, to], y_recv.at[j, k - 1], ry_s, ry_r.at[j],
            device_id=at(x, to, z, core), device_id_type=MESH,
        )

    def take_x(j):
        for k in FAR:
            yb = (y + k) % NY
            blocks = x_recv.at[j, :, yb]
            pltpu.make_async_copy(blocks, blocks, rx_r.at[j, k]).wait()
            total = x_send[j, x, yb].astype(F32)
            for a in range(NX - 1):
                total += x_recv[j, a, yb].astype(F32)
            y_send[j, yb] = total.astype(BF16)
            if k:
                copy_ry(j, k).start()

    def take_y(j):
        pltpu.make_async_copy(y_recv.at[j], y_recv.at[j], ry_r.at[j]).wait()
        total = y_send[j, y].astype(F32)
        for k in range(NY - 1):
            total += y_recv[j, k].astype(F32)
        z_sum[j] = total.astype(BF16)

    def both_cores(j):
        pltpu.make_async_copy(c_recv.at[j], c_recv.at[j], rc_r.at[j]).wait()
        part = dot(h_t[core], gkv[j]).reshape(NX, NY, 32, 128) + c_recv[j].astype(F32)
        x_send[j] = part.astype(BF16)
        for k in FAR:
            for a in (2, 1, 3):
                copy_rx(j, k, a).start()

    def chunk(j, carry):
        wait_core(j)
        kv = jnp.zeros((TOK, 128), F32)
        for xx in range(NX):
            kv += dot(hid[:, xx * 512 : (xx + 1) * 512], natural(w, j, xx))
        kv = kv.astype(BF16)
        s_a[...] = dot(kv[0:128], q_t[j, 0])
        d_a[...] = dot(kv[0:128], c_t[j, 0])
        s_b[...] = dot(kv, q_t[j, 1])
        d_b[...] = dot(kv, c_t[j, 1])

        @pl.when(j > 0)
        def _():
            both_cores(j - 1)

        heads(s_a, d_a, bias_a, p_a, ds_a)
        heads(s_b, d_b, bias_b, p_b, ds_b)

        @pl.when(j < LAST - 1)
        def _():
            wait_x(j + 1)
            copy_core(j + 1).start()

        @pl.when(j == LAST - 1)
        def _():
            wait_then_y()
            copy_core(LAST).start()

        late = dot(ds_b[...], q_n[j, 1]) + dot(p_b[...], c_n[j, 1])
        early = dot(ds_a[...], q_n[j, 0]) + dot(p_a[...], c_n[j, 0])
        grad = jnp.concatenate([late[0:128] + early, late[128:256]], axis=0).astype(BF16)
        gkv[j] = grad
        g_send[j] = dot(h_t[1 - core], grad).astype(BF16).reshape(NX, NY, 32, 128)
        copy_rc(j).start()
        return carry

    lax.fori_loop(0, CH, chunk, 0)

    take_x(0)
    both_cores(LAST)
    take_x(1)
    take_x(2)
    grads = jnp.concatenate([gkv[j] for j in range(CH)], axis=1)

    def hidden_part(xx, carry):
        rows = jnp.concatenate([natural(w, j, xx) for j in range(CH)], axis=1)
        cols = pl.ds(pl.multiple_of(xx * 512, 512), 512)
        gh[:, cols] = lax.dot_general(grads, rows, NT, preferred_element_type=F32).astype(BF16)
        return carry

    lax.fori_loop(0, NX, hidden_part, 0)
    out = pltpu.make_async_copy(gh, gh_hbm, out_sem)
    out.start()

    take_x(CH - 1)
    lax.fori_loop(0, CH, lambda j, carry: (take_y(j), carry)[1], 0)

    back = ((r_out % 16) // 4) * 32 + (r_out // 16) * 4 + r_out % 4
    z_send[...] = (
        dot((r_in == back).astype(BF16), z_sum[...].reshape(128, 128)).astype(BF16).reshape(8, 16, 128)
    )

    def scatter_z(a, b, remote):
        to_h, to_c = (zh + a) % NZH, (core + b) % NC
        piece = z_send.at[to_h * NC + to_c]
        if not remote:
            return pltpu.make_async_copy(piece, f_recv.at[z], rz_r)
        return pltpu.make_async_remote_copy(
            piece, f_recv.at[z], rz_s, rz_r,
            device_id=at(x, y, to_h * NZL + core, to_c), device_id_type=MESH,
        )

    for a in (2, 1, 3, 0):
        for b in range(NC):
            if a or b:
                scatter_z(a, b, True).start()

    @pl.when(home)
    def _():
        scatter_z(0, 0, False).start()

    @pl.when(jnp.logical_not(home))
    def _():
        scatter_z(0, 0, True).start()

    pltpu.make_async_copy(zrecv.at[0:7], zrecv.at[0:7], az_s).wait()

    @pl.when(jnp.logical_not(home))
    def _():
        pltpu.make_async_copy(zrecv.at[0], zrecv.at[0], az_s).wait()

    ay_all, ax_all = y_recv.at[0:LAST], x_recv.at[0:LAST]
    pltpu.make_async_copy(ay_all, ay_all, ay_s).wait()
    pltpu.make_async_copy(ax_all, ax_all, ax_s).wait()
    bx_all, by_all = x_recv.at[0, :, 0], c_recv.at[0, :, 0 : NY - 1]
    pltpu.make_async_copy(bx_all, bx_all, bx_s).wait()
    pltpu.make_async_copy(by_all, by_all, by_s).wait()
    pltpu.make_async_copy(c_recv, c_recv, ac_s).wait()
    pltpu.make_async_copy(c_recv, c_recv, rc_s).wait()
    pltpu.make_async_copy(x_recv, x_recv, rx_s).wait()
    pltpu.make_async_copy(y_recv, y_recv, ry_s).wait()

    out.wait()
    pltpu.make_async_copy(f_recv, f_recv, rz_r).wait()
    total = f_recv[0].astype(F32)
    for k in range(1, 8):
        total += f_recv[k].astype(F32)
    total *= scale
    gw_ref[...] = jnp.concatenate(
        [total[4 * j : 4 * j + 4, side * 64 : side * 64 + 64] for side in range(2) for j in range(CH)], axis=1
    )

    pltpu.make_async_copy(f_recv.at[0:7], f_recv.at[0:7], rz_s).wait()

    @pl.when(jnp.logical_not(home))
    def _():
        pltpu.make_async_copy(f_recv.at[0], f_recv.at[0], rz_s).wait()


def on_device(hidden, queries, cotangent, segments, kv_weight):
    hbm = pl.BlockSpec(memory_space=pl.ANY)
    vmem = pl.BlockSpec(memory_space=pltpu.VMEM)
    scale = 1.0 / math.sqrt(lax.axis_size(("dp", "node")) * TOK)
    dma = pltpu.SemaphoreType.DMA
    scratch = [
        ((TOK, 2048), BF16), ((TOK, 1024), BF16), ((TOK, 1024), BF16), ((1, TOK), jnp.int32), ((4, 512), BF16),
        ((16, 128), BF16), ((8, 16, 128), BF16), ((CH, 2, NX, NY, 32, 128), BF16), ((2, 1024, TOK), BF16),
        ((CH, 2, 128, 512), BF16), ((CH, 2, 128, 512), BF16), ((CH, 2, 512, 128), BF16), ((CH, 2, 512, 128), BF16),
        ((128, 128), F32), ((256, 128), F32),
        ((128, 512), F32), ((256, 512), F32), ((128, 512), F32), ((256, 512), F32),
        ((128, 512), BF16), ((256, 512), BF16), ((128, 512), BF16), ((256, 512), BF16), ((CH, TOK, 128), BF16),
        ((CH, NX, NY, 32, 128), BF16), ((CH, NX, NY, 32, 128), BF16),
        ((CH, NX, NY, 32, 128), BF16), ((CH, NX - 1, NY, 32, 128), BF16),
        ((CH, NY, 32, 128), BF16), ((CH, NY - 1, 32, 128), BF16),
        ((CH, 32, 128), BF16), ((8, 16, 128), BF16), ((8, 16, 128), BF16), ((TOK, 2048), BF16),
    ]
    return pl.pallas_call(
        functools.partial(kernel, scale),
        out_shape=(
            jax.ShapeDtypeStruct((TOK, 2048), BF16),
            jax.ShapeDtypeStruct((4, 512), F32),
        ),
        in_specs=[hbm] * 5,
        out_specs=(hbm, vmem),
        scratch_shapes=[pltpu.VMEM(shape, kind) for shape, kind in scratch]
        + [
            dma((5,)), dma,
            dma, dma, dma, dma((LAST, NY - 1)), dma, dma((LAST,)), dma, dma((NX - 1,)), dma, dma, dma, dma((CH,)),
            dma, dma((CH,)), dma, dma((CH, NY)), dma, dma((CH,)), dma, dma,
        ],
        compiler_params=pltpu.CompilerParams(
            collective_id=0, has_side_effects=True, vmem_limit_bytes=40 << 20
        ),
    )(
        *(
            pltpu.with_memory_space_constraint(array, pltpu.HBM)
            for array in (hidden, queries, cotangent, segments, kv_weight)
        )
    )


def solution(mesh):
    placed = P(("dp", "node"), None)
    return jax.shard_map(
        on_device,
        mesh=mesh,
        in_specs=(placed,) * 5,
        out_specs=(placed, placed),
        check_vma=False,
    )
```

```python
import functools
import math

import jax
import jax.numpy as jnp
from jax import lax
from jax.experimental import pallas as pl
from jax.experimental.pallas import tpu as pltpu
from jax.sharding import PartitionSpec as P

HEAD = 64
KV_HEADS = 4
GROUP = 4
TOK = 256
HALF = 128
NX, NY, NZL, NZH, NC = 4, 8, 2, 4, 2
NZC = 16
CH = KV_HEADS
MESH = pl.DeviceIdType.MESH
F32, BF16 = jnp.float32, jnp.bfloat16
NT = (((1,), (1,)), ((), ()))
NEAR = (1, 7, 2, 6, 3, 5, 4)
FAR = (4, 3, 5, 2, 6, 1, 7, 0)
LAST = CH - 1


def dot(a, b):
    return jnp.dot(a, b, preferred_element_type=F32)


def natural(w_ref, j, x):
    both = jnp.stack([w_ref[j, 0, x], w_ref[j, 1, x]], axis=1)
    return both.reshape(512, 128)


def kernel(
    scale,
    hid_hbm, que_hbm, cot_hbm, seg_hbm, kvw_hbm,
    gh, gw_ref,
    hid, que, cot, seg, kvw,
    blk, zrecv, w, h_t, q_t, c_t, q_n, c_n, bias_a, bias_b,
    s_a, s_b, d_a, d_b, p_a, p_b, ds_a, ds_b, gkv,
    g_send, c_recv, x_send, x_recv, y_send, y_recv, z_sum, z_send, f_recv,
    in_sem,
    az_s, az_r, ay_s, ay_r, ax_s, ax_r, bx_s, bx_r, by_s, by_r, ac_s, ac_r,
    rc_s, rc_r, rx_s, rx_r, ry_s, ry_r, rz_s, rz_r,
):
    dp, node = lax.axis_index("dp"), lax.axis_index("node")
    x = dp // (NY * NZL)
    y = (dp // NZL) % NY
    zl = dp % NZL
    zh = node // NC
    core = node % NC
    z = zh * NZL + zl

    def at(x_, y_, z_, c_):
        return ((x_ * NY + y_) * NZL + z_ % NZL, (z_ // NZL) * NC + c_)

    barrier = pltpu.get_barrier_semaphore()

    def greet_z(k):
        other = (z * NC + core + k) % NZC
        pl.semaphore_signal(
            barrier, inc=1, device_id=at(x, y, other // NC, other % NC), device_id_type=MESH
        )

    def greet_y(k):
        pl.semaphore_signal(
            barrier, inc=1, device_id=at(x, (y + k) % NY, z, core), device_id_type=MESH
        )

    def greet_x(k):
        pl.semaphore_signal(
            barrier, inc=1, device_id=at((x + k) % NX, y, z, core), device_id_type=MESH
        )

    for k in (8, 9, 7, 10, 6, 11, 5, 12, 4):
        greet_z(k)
    for k in FAR[:-1]:
        greet_y(k)
    for k in (13, 3, 14, 2, 15, 1):
        greet_z(k)
    for k in (2, 1, 3):
        greet_x(k)

    ins = [
        pltpu.make_async_copy(kvw_hbm, kvw, in_sem.at[0]),
        pltpu.make_async_copy(hid_hbm, hid, in_sem.at[1]),
        pltpu.make_async_copy(que_hbm, que, in_sem.at[2]),
        pltpu.make_async_copy(cot_hbm, cot, in_sem.at[3]),
        pltpu.make_async_copy(seg_hbm, seg, in_sem.at[4]),
    ]
    for cp in ins:
        cp.start()

    ins[0].wait()
    own = kvw[...].astype(F32)
    blk[...] = jnp.concatenate(
        [
            jnp.concatenate([own[:, j * 64 : j * 64 + 64], own[:, 256 + j * 64 : 320 + j * 64]], axis=1)
            for j in range(CH)
        ],
        axis=0,
    ).astype(BF16)
    pl.semaphore_wait(barrier, (NZC - 1) + (NY - 1) + (NX - 1))

    slot = zh * NC + core

    def gather_z(a, b, remote):
        if not remote:
            return pltpu.make_async_copy(blk, zrecv.at[slot], az_r)
        return pltpu.make_async_remote_copy(
            blk, zrecv.at[slot], az_s, az_r,
            device_id=at(x, y, ((zh + a) % NZH) * NZL + (zl + b) % NZL, zl), device_id_type=MESH,
        )

    for a in range(NZH):
        for b in range(NZL):
            if a or b:
                gather_z(a, b, True).start()
    home = core == zl

    @pl.when(home)
    def _():
        gather_z(0, 0, False).start()

    @pl.when(jnp.logical_not(home))
    def _():
        gather_z(0, 0, True).start()

    ins[1].wait()
    for t in range(16):
        cols = hid[:, t * 128 : (t + 1) * 128].astype(F32)
        turned = jnp.transpose(cols).astype(BF16)
        for half in range(4):
            row = t * 2 + half // 2
            h_t[half % 2, row * 32 : row * 32 + 32, :] = turned[half * 32 : half * 32 + 32, :]

    pltpu.make_async_copy(zrecv, zrecv, az_r).wait()
    r_out = lax.broadcasted_iota(jnp.int32, (128, 128), 0)
    r_in = lax.broadcasted_iota(jnp.int32, (128, 128), 1)
    wanted = ((r_out // 4) % 8) * 16 + (r_out // 32) * 4 + r_out % 4
    mine = dot((r_in == wanted).astype(BF16), zrecv[...].reshape(128, 128)).astype(BF16)
    w[:, core, x, y] = mine.reshape(CH, 32, 128)

    def copy_y(j, k):
        return pltpu.make_async_remote_copy(
            w.at[j, core, x, y], w.at[j, core, x, y], ay_s, ay_r.at[j, k - 1],
            device_id=at(x, (y + k) % NY, z, core), device_id_type=MESH,
        )

    def first_x(a):
        return pltpu.make_async_remote_copy(
            w.at[LAST, core, x, y], w.at[LAST, core, x, y], bx_s, bx_r.at[a - 1],
            device_id=at((x + a) % NX, y, z, core), device_id_type=MESH,
        )

    def wait_first_x(a):
        src = (x + NX - a) % NX
        pltpu.make_async_copy(
            w.at[LAST, core, src, y], w.at[LAST, core, src, y], bx_r.at[a - 1]
        ).wait()

    def then_y(xb, k):
        return pltpu.make_async_remote_copy(
            w.at[LAST, core, xb, y], w.at[LAST, core, xb, y], by_s, by_r,
            device_id=at(x, (y + k) % NY, z, core), device_id_type=MESH,
        )

    def wait_y(j, k):
        src = (y + NY - k) % NY
        pltpu.make_async_copy(
            w.at[j, core, x, src], w.at[j, core, x, src], ay_r.at[j, k - 1]
        ).wait()

    def copy_x(j, yb, a):
        return pltpu.make_async_remote_copy(
            w.at[j, core, x, yb], w.at[j, core, x, yb], ax_s, ax_r.at[j],
            device_id=at((x + a) % NX, y, z, core), device_id_type=MESH,
        )

    def send_y(j, carry):
        for k in NEAR:
            copy_y(j, k).start()
        for a in (2, 1, 3):
            copy_x(j, y, a).start()
        return carry

    lax.fori_loop(0, 1, send_y, 0)
    for a in (2, 1, 3):
        first_x(a).start()
    lax.fori_loop(1, LAST, send_y, 0)
    for k in NEAR:
        then_y(x, k).start()

    ins[2].wait()
    ins[3].wait()
    lane = lax.broadcasted_iota(jnp.int32, (TOK, 128), 1)
    low = lane < 64
    zeros = jnp.zeros((64, 512), BF16)
    for j in range(CH):
        for part in range(2):
            q_t[j, part, 64:128, :] = zeros
            c_t[j, part, 0:64, :] = zeros
        for pair in range(2):
            tile = j * 2 + pair
            q = que[:, tile * 128 : (tile + 1) * 128].astype(F32) * 0.125
            c = cot[:, tile * 128 : (tile + 1) * 128].astype(F32)
            q_turn, c_turn = jnp.transpose(q).astype(BF16), jnp.transpose(c).astype(BF16)
            q_swap, c_swap = pltpu.roll(q, 64, 1), pltpu.roll(c, 64, 1)
            q_rows = (jnp.where(low, q, 0.0).astype(BF16), jnp.where(low, q_swap, 0.0).astype(BF16))
            c_rows = (jnp.where(low, 0.0, c_swap).astype(BF16), jnp.where(low, 0.0, c).astype(BF16))
            for side in range(2):
                g = pair * 2 + side
                for part in range(2):
                    toks = slice(part * 128, part * 128 + 128)
                    lanes = slice(g * 128, g * 128 + 128)
                    q_t[j, part, 0:64, lanes] = q_turn[side * 64 : side * 64 + 64, toks]
                    c_t[j, part, 64:128, lanes] = c_turn[side * 64 : side * 64 + 64, toks]
                    q_n[j, part, lanes, :] = q_rows[side][toks, :]
                    c_n[j, part, lanes, :] = c_rows[side][toks, :]

    def forward(j, carry):
        for k in NEAR:
            wait_y(j, k)
            for a in (2, 1, 3):
                copy_x(j, (y + NY - k) % NY, a).start()
        return carry

    lax.fori_loop(0, 1, forward, 0)
    for a in (1, 3, 2):
        wait_first_x(a)
        for k in NEAR:
            then_y((x + NX - a) % NX, k).start()
    lax.fori_loop(1, LAST, forward, 0)

    ins[4].wait()
    seg_i = jnp.broadcast_to(seg[...].astype(F32), (TOK, TOK))
    seg_j = jnp.transpose(seg_i)
    pos_j = lax.broadcasted_iota(jnp.int32, (TOK, TOK), 0)
    pos_i = lax.broadcasted_iota(jnp.int32, (TOK, TOK), 1)
    bias = jnp.where((seg_i == seg_j) & (pos_i >= pos_j), 0.0, -1e30)
    bias_a[...] = bias[0:128, 0:128]
    bias_b[...] = bias[:, 128:256]

    def wait_x(j):
        pltpu.make_async_copy(w.at[j, core, 0:3], w.at[j, core, 0:3], ax_r.at[j]).wait()

    def wait_then_y():
        blocks = w.at[LAST, core, :, 0 : NY - 1]
        pltpu.make_async_copy(blocks, blocks, by_r).wait()

    def other_core():
        return at(x, y, z, 1 - core)

    def copy_core(j):
        return pltpu.make_async_remote_copy(
            w.at[j, core], w.at[j, core], ac_s, ac_r.at[j],
            device_id=other_core(), device_id_type=MESH,
        )

    def wait_core(j):
        pltpu.make_async_copy(w.at[j, 1 - core], w.at[j, 1 - core], ac_r.at[j]).wait()

    wait_x(0)
    copy_core(0).start()

    def heads(s_ref, d_ref, b_ref, p_ref, o_ref):
        for g in range(GROUP):
            lanes = slice(g * 128, g * 128 + 128)
            s = s_ref[:, lanes] + b_ref[...]
            e = jnp.exp(s - jnp.max(s, axis=0, keepdims=True))
            p = e * (1.0 / jnp.sum(e, axis=0, keepdims=True))
            pb = p.astype(BF16)
            d = d_ref[:, lanes]
            delta = jnp.sum(pb.astype(F32) * d, axis=0, keepdims=True)
            p_ref[:, lanes] = pb
            o_ref[:, lanes] = (p * (d - delta)).astype(BF16)

    def copy_rc(j):
        return pltpu.make_async_remote_copy(
            g_send.at[j], c_recv.at[j], rc_s, rc_r.at[j],
            device_id=other_core(), device_id_type=MESH,
        )

    def copy_rx(j, k, a):
        to, yb = (x + a) % NX, (y + k) % NY
        return pltpu.make_async_remote_copy(
            x_send.at[j, to, yb], x_recv.at[j, a - 1, yb], rx_s, rx_r.at[j, k],
            device_id=at(to, y, z, core), device_id_type=MESH,
        )

    def copy_ry(j, k):
        to = (y + k) % NY
        return pltpu.make_async_remote_copy(
            y_send.at[j, to], y_recv.at[j, k - 1], ry_s, ry_r.at[j],
            device_id=at(x, to, z, core), device_id_type=MESH,
        )

    def take_x(j):
        for k in FAR:
            yb = (y + k) % NY
            blocks = x_recv.at[j, :, yb]
            pltpu.make_async_copy(blocks, blocks, rx_r.at[j, k]).wait()
            total = x_send[j, x, yb].astype(F32)
            for a in range(NX - 1):
                total += x_recv[j, a, yb].astype(F32)
            y_send[j, yb] = total.astype(BF16)
            if k:
                copy_ry(j, k).start()

    def take_y(j):
        pltpu.make_async_copy(y_recv.at[j], y_recv.at[j], ry_r.at[j]).wait()
        total = y_send[j, y].astype(F32)
        for k in range(NY - 1):
            total += y_recv[j, k].astype(F32)
        z_sum[j] = total.astype(BF16)

    def both_cores(j):
        pltpu.make_async_copy(c_recv.at[j], c_recv.at[j], rc_r.at[j]).wait()
        part = dot(h_t[core], gkv[j]).reshape(NX, NY, 32, 128) + c_recv[j].astype(F32)
        x_send[j] = part.astype(BF16)
        for k in FAR:
            for a in (2, 1, 3):
                copy_rx(j, k, a).start()

    def chunk(j, carry):
        wait_core(j)
        kv = jnp.zeros((TOK, 128), F32)
        for xx in range(NX):
            kv += dot(hid[:, xx * 512 : (xx + 1) * 512], natural(w, j, xx))
        kv = kv.astype(BF16)
        s_a[...] = dot(kv[0:128], q_t[j, 0])
        d_a[...] = dot(kv[0:128], c_t[j, 0])
        s_b[...] = dot(kv, q_t[j, 1])
        d_b[...] = dot(kv, c_t[j, 1])

        @pl.when(j > 0)
        def _():
            both_cores(j - 1)

        heads(s_a, d_a, bias_a, p_a, ds_a)
        heads(s_b, d_b, bias_b, p_b, ds_b)

        @pl.when(j < LAST - 1)
        def _():
            wait_x(j + 1)
            copy_core(j + 1).start()

        @pl.when(j == LAST - 1)
        def _():
            wait_then_y()
            copy_core(LAST).start()

        late = dot(ds_b[...], q_n[j, 1]) + dot(p_b[...], c_n[j, 1])
        early = dot(ds_a[...], q_n[j, 0]) + dot(p_a[...], c_n[j, 0])
        grad = jnp.concatenate([late[0:128] + early, late[128:256]], axis=0).astype(BF16)
        gkv[j] = grad
        g_send[j] = dot(h_t[1 - core], grad).astype(BF16).reshape(NX, NY, 32, 128)
        copy_rc(j).start()
        return carry

    lax.fori_loop(0, CH, chunk, 0)

    take_x(0)
    both_cores(LAST)
    take_x(1)
    take_x(2)
    grads = jnp.concatenate([gkv[j] for j in range(CH)], axis=1)

    def hidden_part(xx, carry):
        rows = jnp.concatenate([natural(w, j, xx) for j in range(CH)], axis=1)
        cols = pl.ds(pl.multiple_of(xx * 512, 512), 512)
        gh[:, cols] = lax.dot_general(grads, rows, NT, preferred_element_type=F32).astype(BF16)
        return carry

    lax.fori_loop(0, NX, hidden_part, 0)

    take_x(CH - 1)
    lax.fori_loop(0, CH, lambda j, carry: (take_y(j), carry)[1], 0)

    back = ((r_out % 16) // 4) * 32 + (r_out // 16) * 4 + r_out % 4
    z_send[...] = (
        dot((r_in == back).astype(BF16), z_sum[...].reshape(128, 128)).astype(BF16).reshape(8, 16, 128)
    )

    def scatter_z(a, b, remote):
        to_h, to_c = (zh + a) % NZH, (core + b) % NC
        piece = z_send.at[to_h * NC + to_c]
        if not remote:
            return pltpu.make_async_copy(piece, f_recv.at[z], rz_r)
        return pltpu.make_async_remote_copy(
            piece, f_recv.at[z], rz_s, rz_r,
            device_id=at(x, y, to_h * NZL + core, to_c), device_id_type=MESH,
        )

    for a in (2, 1, 3, 0):
        for b in range(NC):
            if a or b:
                scatter_z(a, b, True).start()

    @pl.when(home)
    def _():
        scatter_z(0, 0, False).start()

    @pl.when(jnp.logical_not(home))
    def _():
        scatter_z(0, 0, True).start()

    pltpu.make_async_copy(zrecv.at[0:7], zrecv.at[0:7], az_s).wait()

    @pl.when(jnp.logical_not(home))
    def _():
        pltpu.make_async_copy(zrecv.at[0], zrecv.at[0], az_s).wait()

    ay_all, ax_all = y_recv.at[0:LAST], x_recv.at[0:LAST]
    pltpu.make_async_copy(ay_all, ay_all, ay_s).wait()
    pltpu.make_async_copy(ax_all, ax_all, ax_s).wait()
    bx_all, by_all = x_recv.at[0, :, 0], c_recv.at[0, :, 0 : NY - 1]
    pltpu.make_async_copy(bx_all, bx_all, bx_s).wait()
    pltpu.make_async_copy(by_all, by_all, by_s).wait()
    pltpu.make_async_copy(c_recv, c_recv, ac_s).wait()
    pltpu.make_async_copy(c_recv, c_recv, rc_s).wait()
    pltpu.make_async_copy(x_recv, x_recv, rx_s).wait()
    pltpu.make_async_copy(y_recv, y_recv, ry_s).wait()

    pltpu.make_async_copy(f_recv, f_recv, rz_r).wait()
    total = f_recv[0].astype(F32)
    for k in range(1, 8):
        total += f_recv[k].astype(F32)
    total *= scale
    gw_ref[...] = jnp.concatenate(
        [total[4 * j : 4 * j + 4, side * 64 : side * 64 + 64] for side in range(2) for j in range(CH)], axis=1
    )

    pltpu.make_async_copy(f_recv.at[0:7], f_recv.at[0:7], rz_s).wait()

    @pl.when(jnp.logical_not(home))
    def _():
        pltpu.make_async_copy(f_recv.at[0], f_recv.at[0], rz_s).wait()


def on_device(hidden, queries, cotangent, segments, kv_weight):
    hbm = pl.BlockSpec(memory_space=pl.ANY)
    vmem = pl.BlockSpec(memory_space=pltpu.VMEM)
    scale = 1.0 / math.sqrt(lax.axis_size(("dp", "node")) * TOK)
    dma = pltpu.SemaphoreType.DMA
    scratch = [
        ((TOK, 2048), BF16), ((TOK, 1024), BF16), ((TOK, 1024), BF16), ((1, TOK), jnp.int32), ((4, 512), BF16),
        ((16, 128), BF16), ((8, 16, 128), BF16), ((CH, 2, NX, NY, 32, 128), BF16), ((2, 1024, TOK), BF16),
        ((CH, 2, 128, 512), BF16), ((CH, 2, 128, 512), BF16), ((CH, 2, 512, 128), BF16), ((CH, 2, 512, 128), BF16),
        ((128, 128), F32), ((256, 128), F32),
        ((128, 512), F32), ((256, 512), F32), ((128, 512), F32), ((256, 512), F32),
        ((128, 512), BF16), ((256, 512), BF16), ((128, 512), BF16), ((256, 512), BF16), ((CH, TOK, 128), BF16),
        ((CH, NX, NY, 32, 128), BF16), ((CH, NX, NY, 32, 128), BF16),
        ((CH, NX, NY, 32, 128), BF16), ((CH, NX - 1, NY, 32, 128), BF16),
        ((CH, NY, 32, 128), BF16), ((CH, NY - 1, 32, 128), BF16),
        ((CH, 32, 128), BF16), ((8, 16, 128), BF16), ((8, 16, 128), BF16),
    ]
    return pl.pallas_call(
        functools.partial(kernel, scale),
        out_shape=(
            jax.ShapeDtypeStruct((TOK, 2048), BF16),
            jax.ShapeDtypeStruct((4, 512), F32),
        ),
        in_specs=[hbm] * 5,
        out_specs=(vmem, vmem),
        scratch_shapes=[pltpu.VMEM(shape, kind) for shape, kind in scratch]
        + [
            dma((5,)),
            dma, dma, dma, dma((LAST, NY - 1)), dma, dma((LAST,)), dma, dma((NX - 1,)), dma, dma, dma, dma((CH,)),
            dma, dma((CH,)), dma, dma((CH, NY)), dma, dma((CH,)), dma, dma,
        ],
        compiler_params=pltpu.CompilerParams(
            collective_id=0, has_side_effects=True, vmem_limit_bytes=40 << 20
        ),
    )(
        *(
            pltpu.with_memory_space_constraint(array, pltpu.HBM)
            for array in (hidden, queries, cotangent, segments, kv_weight)
        )
    )


def solution(mesh):
    placed = P(("dp", "node"), None)
    return jax.shard_map(
        on_device,
        mesh=mesh,
        in_specs=(placed,) * 5,
        out_specs=(placed, placed),
        check_vma=False,
    )
```
